512 devices in a mesh: band: 16 (over z_lo, y), space: 32 (over z_hi, x, core).
Axes of the slice: x: 4, y: 4, z: 16 (z_hi: 4, z_lo: 4; z = z_hi * 4 + z_lo), core: 2. Of those that a mesh axis runs over, the one named last changes fastest.
Arguments:
- occupied: float32 [2, 256, 64, 1024], P(None, 'band', 'space'), may hold values from -6 to 6
- initial: float32 [128, 64, 1024], P('band', 'space'), may hold values from -6 to 6
- right_side: float32 [128, 64, 1024], P('band', 'space'), may hold values from -6 to 6
- potential: float32 [64, 1024], P('space'), may hold values from 0.5 to 2.5
- energies: float32 [128], P('band'), may hold values from -1.5 to -0.2
Outputs:
- response: float32 [128, 64, 1024], P('band', 'space')
- residual: float32 [128, 64, 1024], P('band', 'space')
The draws below stay inside these ranges and needn't reach their ends.
All inputs are finite; a program needn't handle non-finite values.
Results may differ from the reference program's by a relative error of at most 0.0001.
Values sent between devices are 32-bit elements; how exact they have to be, the bound alone decides.
No kernel may reach another device: no remote copies, remote signals or barrier semaphores. Data moves between devices by JAX's collectives and lax.ppermute only.
A program may use at most 64 MiB of HBM per device.

```python
import jax
import jax.numpy as jnp
from jax import lax

BLOCKS = 2
BLOCK = 256
VEC = 128
NY = 32
NZ = 32
ITERS = 2
NX = 64


def level_of(rng, dims, pieces, least, largest):
    def one(axis_at, parts):
        heights = jax.random.uniform(jax.random.fold_in(jax.random.fold_in(rng, 6), axis_at), (parts,), jnp.float32, least / len(pieces), largest / len(pieces))
        return jnp.repeat(jnp.exp(heights), dims[axis_at] // parts).reshape((-1,) + (1,) * (len(dims) - axis_at - 1))

    factor_of = one(*pieces[0])
    for cut in pieces[1:]:
        factor_of = factor_of * one(*cut)
    return factor_of


def centred(stream_key, dims, width, reach, split=(), held_as=jnp.bfloat16):
    entries = jax.random.normal(stream_key, dims, jnp.float32) * width
    if len(split) > 0:
        entries = level_of(stream_key, dims, split, -0.22, 0.18) * entries
    return jnp.clip(entries, min=-reach, max=reach).astype(held_as)


def setup_inputs(seed: int = 0) -> dict:
    arg_keys = jax.random.split(jax.random.key(seed), 6)
    occupied = centred(arg_keys[0], (BLOCKS, BLOCK, NX, NY * NZ), 1.0, 6.0, ((1, 16), (2, 32)), jnp.float32)
    initial = centred(arg_keys[1], (VEC, NX, NY * NZ), 1.0, 6.0, ((0, 16), (1, 32)), jnp.float32)
    right_side = centred(arg_keys[2], (VEC, NX, NY * NZ), 1.0, 6.0, ((0, 16), (1, 32)), jnp.float32)
    potential = jnp.clip(0.5 + 2.0 * jax.random.uniform(arg_keys[3], (NX, NY * NZ), jnp.float32) ** level_of(arg_keys[3], (NX, NY * NZ), ((0, 32),), -0.2, 0.2), 0.5, 2.5)
    energies = jnp.clip(-1.5 + 1.3 * jax.random.uniform(arg_keys[4], (VEC,), jnp.float32) ** level_of(arg_keys[4], (VEC,), ((0, 16),), -0.2, 0.2), -1.5, -0.2)
    return {"occupied": occupied, "initial": initial, "right_side": right_side, "potential": potential, "energies": energies}


def lateral_terms(vectors, z_cells):
    line_length = vectors.shape[-1]
    leading = [(0, 0)] * (vectors.ndim - 1)
    padded = jnp.pad(vectors, leading + [(2 * z_cells, 2 * z_cells)])
    nearest = padded[..., z_cells:z_cells + line_length] + padded[..., 3 * z_cells:3 * z_cells + line_length]
    second = padded[..., 0:line_length] + padded[..., 4 * z_cells:4 * z_cells + line_length]
    padded_z = jnp.pad(vectors, leading + [(2, 2)])
    z_index = jnp.arange(line_length) % z_cells
    nearest = nearest + jnp.where(z_index >= 1, padded_z[..., 1:line_length + 1], 0.0)
    nearest = nearest + jnp.where(z_index <= z_cells - 2, padded_z[..., 3:line_length + 3], 0.0)
    second = second + jnp.where(z_index >= 2, padded_z[..., 0:line_length], 0.0)
    second = second + jnp.where(z_index <= z_cells - 3, padded_z[..., 4:line_length + 4], 0.0)
    return nearest, second


def reference(occupied, initial, right_side, potential, energies):
    vectors = initial
    vector_count, plane_count, line_length = initial.shape
    weight = 1.0 / (plane_count * line_length)
    diagonal = 3.75 + potential[None, :, :] - energies[:, None, None]
    residual = jnp.zeros_like(initial)
    for iteration in range(ITERS):
        for block_index in range(BLOCKS):
            states = occupied[block_index].reshape(occupied.shape[1], -1)
            flattened = vectors.reshape(vector_count, -1)
            margin = jnp.einsum("jc,vc->jv", states, flattened, precision=lax.Precision.HIGHEST,
                                 preferred_element_type=jnp.float32) * weight
            correction = jnp.einsum("jv,jc->vc", margin, states, precision=lax.Precision.HIGHEST,
                                    preferred_element_type=jnp.float32)
            vectors = (flattened - correction).reshape(initial.shape)
        padded_x = jnp.pad(vectors, ((0, 0), (2, 2), (0, 0)))
        nearest = padded_x[:, 1:plane_count + 1] + padded_x[:, 3:plane_count + 3]
        second = padded_x[:, 0:plane_count] + padded_x[:, 4:plane_count + 4]
        inner_near, inner_second = lateral_terms(vectors, NZ)
        applied = diagonal * vectors - (2.0 / 3.0) * (nearest + inner_near) + (second + inner_second) / 24.0
        residual = right_side - applied
        vectors = vectors + residual / diagonal
    return vectors, residual
```

```python
import jax
import jax.numpy as jnp
from jax import lax
from jax.sharding import PartitionSpec as P

NZ = 32
ITERS = 2
BAND_Z = [[z * 4 + y for z in range(4)] for y in range(4)]
BAND_Y = [[z * 4 + y for y in range(4)] for z in range(4)]
SPACE_PLANE = [[z * 8 + r for r in range(8)] for z in range(4)]
SPACE_Z = [[z * 8 + r for z in range(4)] for r in range(8)]


def copies(x, axis, groups):
    count = len(groups[0])
    sent = jnp.broadcast_to(x[None], (count,) + x.shape)
    return lax.all_to_all(sent, axis, 0, 0, axis_index_groups=groups)


def gathered(states):
    columns = copies(states, "band", BAND_Z)
    return copies(columns, "band", BAND_Y).reshape(-1, states.shape[-1])


def space_sum(x):
    near = jnp.sum(copies(x, "space", SPACE_PLANE), axis=0)
    return lax.psum(near, "space", axis_index_groups=SPACE_Z)


def products(vectors, states):
    return jnp.einsum(
        "vc,jc->vj",
        vectors,
        states,
        precision=lax.Precision.HIGH,
        preferred_element_type=jnp.float32,
    )


def combination(margin, states):
    return jnp.einsum(
        "vj,jc->vc",
        margin,
        states,
        precision=lax.Precision.HIGH,
        preferred_element_type=jnp.float32,
    )


def neighbours(vectors):
    count = lax.axis_size("space")
    outer = [(i, i + 1) for i in range(1, count - 1, 2)]
    outer = outer + [(j, i) for i, j in outer]
    across = lax.ppermute(vectors, "space", outer)
    inside = lax.ppermute(vectors, "space", [(i, i ^ 1) for i in range(count)])
    first = lax.axis_index("space") % 2 == 0
    return jnp.where(first, across, inside), jnp.where(first, inside, across)


def shifted(planes, by):
    length = planes.shape[-1]
    pad = [(0, 0)] * (planes.ndim - 1)
    if by > 0:
        return jnp.pad(planes[..., by:], pad + [(0, by)])
    return jnp.pad(planes[..., :length + by], pad + [(-by, 0)])


def coupling(vectors, low, high):
    z = jnp.arange(vectors.shape[-1]) % NZ
    nearest = shifted(vectors, NZ) + shifted(vectors, -NZ)
    second = shifted(vectors, 2 * NZ) + shifted(vectors, -2 * NZ)
    nearest = nearest + jnp.where(z >= 1, shifted(vectors, -1), 0.0)
    nearest = nearest + jnp.where(z <= NZ - 2, shifted(vectors, 1), 0.0)
    second = second + jnp.where(z >= 2, shifted(vectors, -2), 0.0)
    second = second + jnp.where(z <= NZ - 3, shifted(vectors, 2), 0.0)
    x = jnp.concatenate([low, vectors, high], axis=1)
    nearest = nearest + x[:, 1:3] + x[:, 3:5]
    second = second + x[:, 0:2] + x[:, 4:6]
    return second / 24.0 - 2.0 / 3.0 * nearest


def on_device(occupied, initial, right_side, potential, energies):
    count, planes, line = initial.shape
    weight = 1.0 / (planes * lax.axis_size("space") * line)
    states = [occupied[0].reshape(-1, planes * line), occupied[1].reshape(-1, planes * line)]
    later = lax.all_gather(states[1], "band", axis=0, tiled=True)
    blocks = [gathered(states[0]), later]
    diagonal = 3.75 + potential[None, :, :] - energies[:, None, None]
    vectors = initial.reshape(count, planes * line)
    for iteration in range(ITERS):
        for block in blocks:
            margin = space_sum(products(vectors, block)) * weight
            vectors = vectors - combination(margin, block)
        low, high = neighbours(vectors)
        shape = (count, planes, line)
        vectors = vectors.reshape(shape)
        rest = right_side - coupling(vectors, low.reshape(shape), high.reshape(shape))
        residual = rest - diagonal * vectors
        vectors = (rest / diagonal).reshape(count, planes * line)
    return (vectors.reshape(shape), residual)


def solution(mesh):
    return jax.shard_map(
        on_device,
        mesh=mesh,
        in_specs=(
            P(None, "band", "space", None),
            P("band", "space", None),
            P("band", "space", None),
            P("space", None),
            P("band"),
        ),
        out_specs=(P("band", "space", None), P("band", "space", None)),
        check_vma=False,
    )
```

```python
import jax
import jax.numpy as jnp
from jax import lax
from jax.sharding import PartitionSpec as P

NZ = 32
ITERS = 2
BAND_Z = [[z * 4 + y for z in range(4)] for y in range(4)]
BAND_Y = [[z * 4 + y for y in range(4)] for z in range(4)]
SPACE_X = [[z * 8 + x * 2 + c for x in range(4)] for z in range(4) for c in range(2)]
SPACE_Z = [[z * 8 + r for z in range(4)] for r in range(8)]


def copies(x, axis, groups):
    count = len(groups[0])
    sent = jnp.broadcast_to(x[None], (count,) + x.shape)
    return lax.all_to_all(sent, axis, 0, 0, axis_index_groups=groups)


def gathered(states):
    return copies(copies(states, "band", BAND_Z), "band", BAND_Y)


def space_sum(x):
    half = x.shape[0] // 2
    flip = [(i, i ^ 1) for i in range(lax.axis_size("space"))]
    upper = lax.axis_index("space") % 2 == 1
    lower_half, upper_half = x[:half], x[half:]
    kept = jnp.where(upper, upper_half, lower_half)
    kept = kept + lax.ppermute(jnp.where(upper, lower_half, upper_half), "space", flip)
    if kept.size <= 2048:
        kept = lax.psum(kept, "space", axis_index_groups=SPACE_X)
        kept = lax.psum(kept, "space", axis_index_groups=SPACE_Z)
    else:
        kept = jnp.sum(copies(kept, "space", SPACE_X), axis=0)
        kept = jnp.sum(copies(kept, "space", SPACE_Z), axis=0)
    other = lax.ppermute(kept, "space", flip)
    return jnp.concatenate(
        [jnp.where(upper, other, kept), jnp.where(upper, kept, other)], axis=0
    )


def products(vectors, states):
    return jnp.einsum(
        "vc,jc->vj",
        vectors,
        states,
        precision=lax.Precision.HIGH,
        preferred_element_type=jnp.float32,
    )


def combination(margin, states):
    return jnp.einsum(
        "vj,jc->vc",
        margin,
        states,
        precision=lax.Precision.HIGH,
        preferred_element_type=jnp.float32,
    )


def neighbours(vectors):
    count = lax.axis_size("space")
    outer = [(i, i + 1) for i in range(1, count - 1, 2)]
    outer = outer + [(j, i) for i, j in outer]
    across = lax.ppermute(vectors, "space", outer)
    inside = lax.ppermute(vectors, "space", [(i, i ^ 1) for i in range(count)])
    first = lax.axis_index("space") % 2 == 0
    return jnp.where(first, across, inside), jnp.where(first, inside, across)


def shifted(planes, by):
    length = planes.shape[-1]
    pad = [(0, 0)] * (planes.ndim - 1)
    if by > 0:
        return jnp.pad(planes[..., by:], pad + [(0, by)])
    return jnp.pad(planes[..., :length + by], pad + [(-by, 0)])


def coupling(vectors, low, high):
    z = jnp.arange(vectors.shape[-1]) % NZ
    nearest = shifted(vectors, NZ) + shifted(vectors, -NZ)
    second = shifted(vectors, 2 * NZ) + shifted(vectors, -2 * NZ)
    nearest = nearest + jnp.where(z >= 1, shifted(vectors, -1), 0.0)
    nearest = nearest + jnp.where(z <= NZ - 2, shifted(vectors, 1), 0.0)
    second = second + jnp.where(z >= 2, shifted(vectors, -2), 0.0)
    second = second + jnp.where(z <= NZ - 3, shifted(vectors, 2), 0.0)
    x = jnp.concatenate([low, vectors, high], axis=1)
    nearest = nearest + x[:, 1:3] + x[:, 3:5]
    second = second + x[:, 0:2] + x[:, 4:6]
    return second / 24.0 - 2.0 / 3.0 * nearest


def on_device(occupied, initial, right_side, potential, energies):
    count, planes, line = initial.shape
    cells = planes * line
    weight = 1.0 / (lax.axis_size("space") * cells)
    block = occupied.shape[1]
    states = occupied.reshape(2 * block, cells)
    part = block + block // 2
    last = lax.all_gather(states[part:], "band", axis=0, tiled=True)
    most = gathered(states[:part]).reshape(16, part, cells)
    first = most[:, :block].reshape(-1, cells)
    middle = most[:, block:].reshape(-1, cells)
    diagonal = 3.75 + potential[None, :, :] - energies[:, None, None]
    vectors = initial.reshape(count, cells)
    overlap_middle = overlap_last = None
    for iteration in range(ITERS):
        raw_second = jnp.concatenate(
            [products(vectors, middle), products(vectors, last)], axis=1
        )
        if iteration == 0:
            raw = products(jnp.concatenate([vectors, states[block:]], axis=0), first)
            total = space_sum(
                weight * jnp.concatenate([raw[:count], raw_second, raw[count:]], axis=0)
            )
            rows = lax.all_to_all(
                jnp.broadcast_to(total[None, 2 * count :], (16, block, total.shape[1])),
                "band", 0, 0,
            )
            overlap_last = rows[:, block // 2 :].reshape(-1, total.shape[1])
            rows = rows[:, : block // 2].reshape(4, 4, block // 2, total.shape[1])
            overlap_middle = jnp.swapaxes(rows, 0, 1).reshape(-1, total.shape[1])
        else:
            raw = products(vectors, first)
            total = space_sum(weight * jnp.concatenate([raw, raw_second], axis=0))
        margin = total[:count]
        middle_count = middle.shape[0]
        margin_middle = total[count : 2 * count, :middle_count] - products(margin, overlap_middle)
        margin_last = total[count : 2 * count, middle_count:] - products(margin, overlap_last)
        vectors = (
            vectors
            - combination(margin, first)
            - combination(margin_middle, middle)
            - combination(margin_last, last)
        )
        low, high = neighbours(vectors)
        shape = (count, planes, line)
        vectors = vectors.reshape(shape)
        rest = right_side - coupling(vectors, low.reshape(shape), high.reshape(shape))
        residual = rest - diagonal * vectors
        vectors = (rest / diagonal).reshape(count, cells)
    return (vectors.reshape(shape), residual)


def solution(mesh):
    return jax.shard_map(
        on_device,
        mesh=mesh,
        in_specs=(
            P(None, "band", "space", None),
            P("band", "space", None),
            P("band", "space", None),
            P("space", None),
            P("band"),
        ),
        out_specs=(P("band", "space", None), P("band", "space", None)),
        check_vma=False,
    )
```

```python
import jax
import jax.numpy as jnp
from jax import lax
from jax.sharding import PartitionSpec as P

NZ = 32
ITERS = 2
BAND_Z = [[z * 4 + y for z in range(4)] for y in range(4)]
BAND_Y = [[z * 4 + y for y in range(4)] for z in range(4)]
SPACE_PLANE = [[z * 8 + r for r in range(8)] for z in range(4)]
SPACE_Z = [[z * 8 + r for z in range(4)] for r in range(8)]


def copies(x, axis, groups):
    count = len(groups[0])
    sent = jnp.broadcast_to(x[None], (count,) + x.shape)
    return lax.all_to_all(sent, axis, 0, 0, axis_index_groups=groups)


def space_sum(x):
    near = jnp.sum(copies(x, "space", SPACE_PLANE), axis=0)
    return lax.psum(near, "space", axis_index_groups=SPACE_Z)


def products(vectors, states):
    return jnp.einsum(
        "vc,jc->vj",
        vectors,
        states,
        precision=lax.Precision.HIGH,
        preferred_element_type=jnp.float32,
    )


def combination(margin, states):
    return jnp.einsum(
        "vj,jc->vc",
        margin,
        states,
        precision=lax.Precision.HIGH,
        preferred_element_type=jnp.float32,
    )


def neighbours(vectors):
    count = lax.axis_size("space")
    outer = [(i, i + 1) for i in range(1, count - 1, 2)]
    outer = outer + [(j, i) for i, j in outer]
    across = lax.ppermute(vectors, "space", outer)
    inside = lax.ppermute(vectors, "space", [(i, i ^ 1) for i in range(count)])
    first = lax.axis_index("space") % 2 == 0
    return jnp.where(first, across, inside), jnp.where(first, inside, across)


def shifted(planes, by):
    length = planes.shape[-1]
    pad = [(0, 0)] * (planes.ndim - 1)
    if by > 0:
        return jnp.pad(planes[..., by:], pad + [(0, by)])
    return jnp.pad(planes[..., :length + by], pad + [(-by, 0)])


def coupling(vectors, low, high):
    z = jnp.arange(vectors.shape[-1]) % NZ
    nearest = shifted(vectors, NZ) + shifted(vectors, -NZ)
    second = shifted(vectors, 2 * NZ) + shifted(vectors, -2 * NZ)
    nearest = nearest + jnp.where(z >= 1, shifted(vectors, -1), 0.0)
    nearest = nearest + jnp.where(z <= NZ - 2, shifted(vectors, 1), 0.0)
    second = second + jnp.where(z >= 2, shifted(vectors, -2), 0.0)
    second = second + jnp.where(z <= NZ - 3, shifted(vectors, 2), 0.0)
    x = jnp.concatenate([low, vectors, high], axis=1)
    nearest = nearest + x[:, 1:3] + x[:, 3:5]
    second = second + x[:, 0:2] + x[:, 4:6]
    return second / 24.0 - 2.0 / 3.0 * nearest


def project_shared(states, vectors, weight):
    count, cells = vectors.shape
    run = copies(vectors, "band", BAND_Z).reshape(-1, cells)
    half = run.shape[0] // 2
    product = products(run, states)
    margin = space_sum(jnp.concatenate([product[:half], product[half:]], axis=1)) * weight
    width = states.shape[0]
    margin = jnp.concatenate([margin[:, :width], margin[:, width:]], axis=0)
    partial = combination(margin, states).reshape(-1, count, cells)
    partial = lax.all_to_all(partial, "band", 0, 0, axis_index_groups=BAND_Z)
    return vectors - jnp.sum(partial, axis=0)


def project_whole(states, vectors, weight):
    margin = space_sum(products(vectors, states)) * weight
    return vectors - combination(margin, states)


def on_device(occupied, initial, right_side, potential, energies):
    count, planes, line = initial.shape
    cells = planes * line
    weight = 1.0 / (lax.axis_size("space") * cells)
    blocks, own = occupied.shape[:2]
    states = occupied.reshape(blocks, own, cells)
    whole = lax.all_gather(states, "band", axis=1, tiled=True)
    ring = copies(states, "band", BAND_Y)
    diagonal = 3.75 + potential[None, :, :] - energies[:, None, None]
    vectors = initial.reshape(count, cells)
    for iteration in range(ITERS):
        for block in range(blocks):
            if iteration == 0:
                vectors = project_shared(ring[:, block].reshape(-1, cells), vectors, weight)
            else:
                vectors = project_whole(whole[block], vectors, weight)
        low, high = neighbours(vectors)
        shape = (count, planes, line)
        vectors = vectors.reshape(shape)
        rest = right_side - coupling(vectors, low.reshape(shape), high.reshape(shape))
        residual = rest - diagonal * vectors
        vectors = (rest / diagonal).reshape(count, cells)
    return (vectors.reshape(shape), residual)


def solution(mesh):
    return jax.shard_map(
        on_device,
        mesh=mesh,
        in_specs=(
            P(None, "band", "space", None),
            P("band", "space", None),
            P("band", "space", None),
            P("space", None),
            P("band"),
        ),
        out_specs=(P("band", "space", None), P("band", "space", None)),
        check_vma=False,
    )
```

```python
import jax
import jax.numpy as jnp
from jax import lax
from jax.sharding import PartitionSpec as P

NZ = 32
ITERS = 2
BAND_Z = [[z * 4 + y for z in range(4)] for y in range(4)]
BAND_Y = [[z * 4 + y for y in range(4)] for z in range(4)]
SPACE_PLANE = [[z * 8 + r for r in range(8)] for z in range(4)]
SPACE_Z = [[z * 8 + r for z in range(4)] for r in range(8)]


def copies(x, axis, groups):
    count = len(groups[0])
    sent = jnp.broadcast_to(x[None], (count,) + x.shape)
    return lax.all_to_all(sent, axis, 0, 0, axis_index_groups=groups)


def space_sum(x):
    near = jnp.sum(copies(x, "space", SPACE_PLANE), axis=0)
    return lax.psum(near, "space", axis_index_groups=SPACE_Z)


def products(vectors, states):
    return jnp.einsum(
        "vc,jc->vj",
        vectors,
        states,
        precision=lax.Precision.HIGH,
        preferred_element_type=jnp.float32,
    )


def combination(margin, states):
    return jnp.einsum(
        "vj,jc->vc",
        margin,
        states,
        precision=lax.Precision.HIGH,
        preferred_element_type=jnp.float32,
    )


def neighbours(vectors):
    count = lax.axis_size("space")
    outer = [(i, i + 1) for i in range(1, count - 1, 2)]
    outer = outer + [(j, i) for i, j in outer]
    across = lax.ppermute(vectors, "space", outer)
    inside = lax.ppermute(vectors, "space", [(i, i ^ 1) for i in range(count)])
    first = lax.axis_index("space") % 2 == 0
    return jnp.where(first, across, inside), jnp.where(first, inside, across)


def shifted(planes, by):
    length = planes.shape[-1]
    pad = [(0, 0)] * (planes.ndim - 1)
    if by > 0:
        return jnp.pad(planes[..., by:], pad + [(0, by)])
    return jnp.pad(planes[..., :length + by], pad + [(-by, 0)])


def coupling(vectors, low, high):
    z = jnp.arange(vectors.shape[-1]) % NZ
    nearest = shifted(vectors, NZ) + shifted(vectors, -NZ)
    second = shifted(vectors, 2 * NZ) + shifted(vectors, -2 * NZ)
    nearest = nearest + jnp.where(z >= 1, shifted(vectors, -1), 0.0)
    nearest = nearest + jnp.where(z <= NZ - 2, shifted(vectors, 1), 0.0)
    second = second + jnp.where(z >= 2, shifted(vectors, -2), 0.0)
    second = second + jnp.where(z <= NZ - 3, shifted(vectors, 2), 0.0)
    x = jnp.concatenate([low, vectors, high], axis=1)
    nearest = nearest + x[:, 1:3] + x[:, 3:5]
    second = second + x[:, 0:2] + x[:, 4:6]
    return second / 24.0 - 2.0 / 3.0 * nearest


def on_device(occupied, initial, right_side, potential, energies):
    count, planes, line = initial.shape
    weight = 1.0 / (planes * lax.axis_size("space") * line)
    own = [states.reshape(-1, planes * line) for states in occupied]
    run = copies(own[0], "band", BAND_Z).reshape(-1, planes * line)
    run, other = lax.optimization_barrier((run, own[1]))
    first = copies(run, "band", BAND_Y).reshape(-1, planes * line)
    run = copies(other, "band", BAND_Z).reshape(-1, planes * line)
    later = lax.all_gather(run, "band", axis=0, tiled=True, axis_index_groups=BAND_Y)
    blocks = [first, later]
    diagonal = 3.75 + potential[None, :, :] - energies[:, None, None]
    vectors = initial.reshape(count, planes * line)
    for iteration in range(ITERS):
        for block in blocks:
            margin = space_sum(products(vectors, block)) * weight
            vectors = vectors - combination(margin, block)
        low, high = neighbours(vectors)
        shape = (count, planes, line)
        vectors = vectors.reshape(shape)
        rest = right_side - coupling(vectors, low.reshape(shape), high.reshape(shape))
        residual = rest - diagonal * vectors
        vectors = (rest / diagonal).reshape(count, planes * line)
    return (vectors.reshape(shape), residual)


def solution(mesh):
    return jax.shard_map(
        on_device,
        mesh=mesh,
        in_specs=(
            P(None, "band", "space", None),
            P("band", "space", None),
            P("band", "space", None),
            P("space", None),
            P("band"),
        ),
        out_specs=(P("band", "space", None), P("band", "space", None)),
        check_vma=False,
    )
```

```python
import jax
import jax.numpy as jnp
from jax import lax
from jax.sharding import PartitionSpec as P

NZ = 32
ITERS = 2
BAND_Z = [[z * 4 + y for z in range(4)] for y in range(4)]
BAND_Y = [[z * 4 + y for y in range(4)] for z in range(4)]
SPACE_PLANE = [[z * 8 + r for r in range(8)] for z in range(4)]
SPACE_Z = [[z * 8 + r for z in range(4)] for r in range(8)]


def copies(x, axis, groups):
    count = len(groups[0])
    sent = jnp.broadcast_to(x[None], (count,) + x.shape)
    return lax.all_to_all(sent, axis, 0, 0, axis_index_groups=groups)


def gathered(states):
    columns = copies(states, "band", BAND_Z)
    return copies(columns, "band", BAND_Y).reshape(-1, states.shape[-1])


def space_sum(x):
    near = jnp.sum(copies(x, "space", SPACE_PLANE), axis=0)
    return lax.psum(near, "space", axis_index_groups=SPACE_Z)


def products(vectors, states):
    return jnp.einsum(
        "vc,jc->vj",
        vectors,
        states,
        precision=lax.Precision.HIGH,
        preferred_element_type=jnp.float32,
    )


def combination(margin, states):
    return jnp.einsum(
        "vj,jc->vc",
        margin,
        states,
        precision=lax.Precision.HIGH,
        preferred_element_type=jnp.float32,
    )


def neighbours(vectors):
    count = lax.axis_size("space")
    outer = [(i, i + 1) for i in range(1, count - 1, 2)]
    outer = outer + [(j, i) for i, j in outer]
    across = lax.ppermute(vectors, "space", outer)
    inside = lax.ppermute(vectors, "space", [(i, i ^ 1) for i in range(count)])
    first = lax.axis_index("space") % 2 == 0
    return jnp.where(first, across, inside), jnp.where(first, inside, across)


def stencil_rows(cells, line):
    cell = lax.broadcasted_iota(jnp.int32, (1, cells), 1)
    z = cell % NZ
    y = (cell % line) // NZ
    lines = line // NZ
    rows = []
    for step, factor in ((1, -2.0 / 3.0), (2, 1.0 / 24.0)):
        rows.append((step, jnp.where(z >= step, factor, 0.0)))
        rows.append((-step, jnp.where(z < NZ - step, factor, 0.0)))
        rows.append((step * NZ, jnp.where(y >= step, factor, 0.0)))
        rows.append((-step * NZ, jnp.where(y < lines - step, factor, 0.0)))
    return [shift for shift, _ in rows], [row for _, row in rows]


def across_planes(vectors, low, high, line):
    low0, low1 = low[:, :line], low[:, line:]
    own0, own1 = vectors[:, :line], vectors[:, line:]
    high0, high1 = high[:, :line], high[:, line:]
    return jnp.concatenate(
        [
            (low0 + high0) / 24.0 - 2.0 / 3.0 * (low1 + own1),
            (low1 + high1) / 24.0 - 2.0 / 3.0 * (own0 + high0),
        ],
        axis=1,
    )


def on_device(occupied, initial, right_side, potential, energies):
    count, planes, line = initial.shape
    cells = planes * line
    scale = (lax.axis_size("space") * cells) ** -0.5
    own = [states.reshape(-1, cells) for states in occupied]
    later = lax.all_gather(own[1], "band", axis=0, tiled=True)
    run = copies(own[0], "band", BAND_Z).reshape(-1, cells)
    diagonal = 3.75 + potential.reshape(1, cells) - energies[:, None]
    shifts, rows = stencil_rows(cells, line)
    ready = (initial.reshape(count, cells), right_side.reshape(count, cells), diagonal, 1.0 / diagonal, rows)
    run, ready = lax.optimization_barrier((run, ready))
    vectors, right, diagonal, inverse, rows = ready
    first = lax.optimization_barrier(scale * copies(run, "band", BAND_Y).reshape(-1, cells))
    blocks = [first, None]
    for iteration in range(ITERS):
        for index in range(2):
            if blocks[index] is None:
                vectors, later = lax.optimization_barrier((vectors, later))
                blocks[index] = lax.optimization_barrier(scale * later)
            margin = space_sum(products(vectors, blocks[index]))
            vectors = vectors - combination(margin, blocks[index])
        low, high = neighbours(vectors)
        rest = right
        for shift, row in zip(shifts, rows):
            rest = rest - row * jnp.roll(vectors, shift, axis=1)
        rest = rest - across_planes(vectors, low, high, line)
        residual = rest - diagonal * vectors
        vectors = rest * inverse
    shape = (count, planes, line)
    return (vectors.reshape(shape), residual.reshape(shape))


def solution(mesh):
    return jax.shard_map(
        on_device,
        mesh=mesh,
        in_specs=(
            P(None, "band", "space", None),
            P("band", "space", None),
            P("band", "space", None),
            P("space", None),
            P("band"),
        ),
        out_specs=(P("band", "space", None), P("band", "space", None)),
        check_vma=False,
    )
```

```python
import jax
import jax.numpy as jnp
from jax import lax
from jax.sharding import PartitionSpec as P

NZ = 32
ITERS = 2
BAND_Z = [[z * 4 + y for z in range(4)] for y in range(4)]
BAND_Y = [[z * 4 + y for y in range(4)] for z in range(4)]
SPACE_PLANE = [[z * 8 + r for r in range(8)] for z in range(4)]
SPACE_Z = [[z * 8 + r for z in range(4)] for r in range(8)]


def copies(x, axis, groups):
    count = len(groups[0])
    sent = jnp.broadcast_to(x[None], (count,) + x.shape)
    return lax.all_to_all(sent, axis, 0, 0, axis_index_groups=groups)


def space_sum(x):
    near = jnp.sum(copies(x, "space", SPACE_PLANE), axis=0)
    return lax.psum(near, "space", axis_index_groups=SPACE_Z)


def products(vectors, states):
    return jnp.einsum(
        "vc,jc->vj",
        vectors,
        states,
        precision=lax.Precision.HIGH,
        preferred_element_type=jnp.float32,
    )


def combination(margin, states):
    return jnp.einsum(
        "vj,jc->vc",
        margin,
        states,
        precision=lax.Precision.HIGH,
        preferred_element_type=jnp.float32,
    )


def neighbours(vectors):
    count = lax.axis_size("space")
    outer = [(i, i + 1) for i in range(1, count - 1, 2)]
    outer = outer + [(j, i) for i, j in outer]
    across = lax.ppermute(vectors, "space", outer)
    inside = lax.ppermute(vectors, "space", [(i, i ^ 1) for i in range(count)])
    first = lax.axis_index("space") % 2 == 0
    return jnp.where(first, across, inside), jnp.where(first, inside, across)


def shifted(planes, by):
    length = planes.shape[-1]
    pad = [(0, 0)] * (planes.ndim - 1)
    if by > 0:
        return jnp.pad(planes[..., by:], pad + [(0, by)])
    return jnp.pad(planes[..., :length + by], pad + [(-by, 0)])


def coupling(vectors, low, high):
    z = jnp.arange(vectors.shape[-1]) % NZ
    nearest = shifted(vectors, NZ) + shifted(vectors, -NZ)
    second = shifted(vectors, 2 * NZ) + shifted(vectors, -2 * NZ)
    nearest = nearest + jnp.where(z >= 1, shifted(vectors, -1), 0.0)
    nearest = nearest + jnp.where(z <= NZ - 2, shifted(vectors, 1), 0.0)
    second = second + jnp.where(z >= 2, shifted(vectors, -2), 0.0)
    second = second + jnp.where(z <= NZ - 3, shifted(vectors, 2), 0.0)
    x = jnp.concatenate([low, vectors, high], axis=1)
    nearest = nearest + x[:, 1:3] + x[:, 3:5]
    second = second + x[:, 0:2] + x[:, 4:6]
    return second / 24.0 - 2.0 / 3.0 * nearest


def project_shared(states, vectors, weight):
    count, cells = vectors.shape
    run = copies(vectors, "band", BAND_Z).reshape(-1, cells)
    half = run.shape[0] // 2
    product = products(run, states)
    margin = space_sum(jnp.concatenate([product[:half], product[half:]], axis=1)) * weight
    width = states.shape[0]
    margin = jnp.concatenate([margin[:, :width], margin[:, width:]], axis=0)
    partial = combination(margin, states).reshape(-1, count, cells)
    partial = lax.all_to_all(partial, "band", 0, 0, axis_index_groups=BAND_Z)
    return vectors - jnp.sum(partial, axis=0)


def project_whole(states, vectors, weight):
    margin = space_sum(products(vectors, states)) * weight
    return vectors - combination(margin, states)


def on_device(occupied, initial, right_side, potential, energies):
    count, planes, line = initial.shape
    cells = planes * line
    weight = 1.0 / (lax.axis_size("space") * cells)
    blocks, own = occupied.shape[:2]
    states = occupied.reshape(blocks, own, cells)
    whole = states
    for groups in (BAND_Z, BAND_Y):
        whole = lax.all_gather(whole, "band", axis=1, tiled=True, axis_index_groups=groups)
    ring = copies(states, "band", BAND_Y)
    diagonal = 3.75 + potential[None, :, :] - energies[:, None, None]
    vectors = initial.reshape(count, cells)
    for iteration in range(ITERS):
        for block in range(blocks):
            if iteration == 0:
                vectors = project_shared(ring[:, block].reshape(-1, cells), vectors, weight)
            else:
                vectors = project_whole(whole[block], vectors, weight)
        vectors, whole = lax.optimization_barrier((vectors, whole))
        low, high = neighbours(vectors)
        shape = (count, planes, line)
        vectors = vectors.reshape(shape)
        rest = right_side - coupling(vectors, low.reshape(shape), high.reshape(shape))
        residual = rest - diagonal * vectors
        vectors = (rest / diagonal).reshape(count, cells)
    return (vectors.reshape(shape), residual)


def solution(mesh):
    return jax.shard_map(
        on_device,
        mesh=mesh,
        in_specs=(
            P(None, "band", "space", None),
            P("band", "space", None),
            P("band", "space", None),
            P("space", None),
            P("band"),
        ),
        out_specs=(P("band", "space", None), P("band", "space", None)),
        check_vma=False,
    )
```

```python
import jax
import jax.numpy as jnp
from jax import lax
from jax.sharding import PartitionSpec as P

NZ = 32
ITERS = 2
BAND_Z = [[z * 4 + y for z in range(4)] for y in range(4)]
BAND_Y = [[z * 4 + y for y in range(4)] for z in range(4)]
SPACE_PLANE = [[z * 8 + r for r in range(8)] for z in range(4)]
SPACE_Z = [[z * 8 + r for z in range(4)] for r in range(8)]


def copies(x, axis, groups):
    count = len(groups[0])
    sent = jnp.broadcast_to(x[None], (count,) + x.shape)
    return lax.all_to_all(sent, axis, 0, 0, axis_index_groups=groups)


def space_sum(x, beside=None):
    near = jnp.sum(copies(x, "space", SPACE_PLANE), axis=0)
    near, beside = lax.optimization_barrier((near, beside))
    return lax.psum(near, "space", axis_index_groups=SPACE_Z), beside


def products(vectors, states):
    return jnp.einsum(
        "vc,jc->vj",
        vectors,
        states,
        precision=lax.Precision.HIGH,
        preferred_element_type=jnp.float32,
    )


def combination(margin, states):
    return jnp.einsum(
        "vj,jc->vc",
        margin,
        states,
        precision=lax.Precision.HIGH,
        preferred_element_type=jnp.float32,
    )


def neighbours(vectors):
    count = lax.axis_size("space")
    outer = [(i, i + 1) for i in range(1, count - 1, 2)]
    outer = outer + [(j, i) for i, j in outer]
    across = lax.ppermute(vectors, "space", outer)
    inside = lax.ppermute(vectors, "space", [(i, i ^ 1) for i in range(count)])
    first = lax.axis_index("space") % 2 == 0
    return jnp.where(first, across, inside), jnp.where(first, inside, across)


def shifted(planes, by):
    length = planes.shape[-1]
    pad = [(0, 0)] * (planes.ndim - 1)
    if by > 0:
        return jnp.pad(planes[..., by:], pad + [(0, by)])
    return jnp.pad(planes[..., :length + by], pad + [(-by, 0)])


def coupling(vectors, low, high):
    z = jnp.arange(vectors.shape[-1]) % NZ
    nearest = shifted(vectors, NZ) + shifted(vectors, -NZ)
    second = shifted(vectors, 2 * NZ) + shifted(vectors, -2 * NZ)
    nearest = nearest + jnp.where(z >= 1, shifted(vectors, -1), 0.0)
    nearest = nearest + jnp.where(z <= NZ - 2, shifted(vectors, 1), 0.0)
    second = second + jnp.where(z >= 2, shifted(vectors, -2), 0.0)
    second = second + jnp.where(z <= NZ - 3, shifted(vectors, 2), 0.0)
    x = jnp.concatenate([low, vectors, high], axis=1)
    nearest = nearest + x[:, 1:3] + x[:, 3:5]
    second = second + x[:, 0:2] + x[:, 4:6]
    return second / 24.0 - 2.0 / 3.0 * nearest


def project_shared(states, vectors, weight, beside):
    count, cells = vectors.shape
    run = copies(vectors, "band", BAND_Z).reshape(-1, cells)
    half = run.shape[0] // 2
    product = products(run, states)
    total, beside = space_sum(jnp.concatenate([product[:half], product[half:]], axis=1), beside)
    margin = total * weight
    width = states.shape[0]
    margin = jnp.concatenate([margin[:, :width], margin[:, width:]], axis=0)
    partial = combination(margin, states).reshape(-1, count, cells)
    partial = lax.all_to_all(partial, "band", 0, 0, axis_index_groups=BAND_Z)
    return vectors - jnp.sum(partial, axis=0), beside


def project_whole(states, vectors, weight):
    margin = space_sum(products(vectors, states))[0] * weight
    return vectors - combination(margin, states)


def on_device(occupied, initial, right_side, potential, energies):
    count, planes, line = initial.shape
    cells = planes * line
    weight = 1.0 / (lax.axis_size("space") * cells)
    blocks, own = occupied.shape[:2]
    states = occupied.reshape(blocks, own, cells)
    column = lax.all_gather(states, "band", axis=1, tiled=True, axis_index_groups=BAND_Z)
    ring = copies(states, "band", BAND_Y)
    diagonal = 3.75 + potential[None, :, :] - energies[:, None, None]
    vectors = initial.reshape(count, cells)
    for iteration in range(ITERS):
        for block in range(blocks):
            if iteration == 0:
                vectors, column = project_shared(
                    ring[:, block].reshape(-1, cells), vectors, weight, column
                )
                if block == 0:
                    whole = lax.all_gather(
                        column, "band", axis=1, tiled=True, axis_index_groups=BAND_Y
                    )
                    column = None
            else:
                vectors = project_whole(whole[block], vectors, weight)
        low, high = neighbours(vectors)
        shape = (count, planes, line)
        vectors = vectors.reshape(shape)
        rest = right_side - coupling(vectors, low.reshape(shape), high.reshape(shape))
        residual = rest - diagonal * vectors
        vectors = (rest / diagonal).reshape(count, cells)
    return (vectors.reshape(shape), residual)


def solution(mesh):
    return jax.shard_map(
        on_device,
        mesh=mesh,
        in_specs=(
            P(None, "band", "space", None),
            P("band", "space", None),
            P("band", "space", None),
            P("space", None),
            P("band"),
        ),
        out_specs=(P("band", "space", None), P("band", "space", None)),
        check_vma=False,
    )
```

```python
import jax
import jax.numpy as jnp
from jax import lax
from jax.sharding import PartitionSpec as P

NZ = 32
ITERS = 2
BAND_Z = [[z * 4 + y for z in range(4)] for y in range(4)]
BAND_Y = [[z * 4 + y for y in range(4)] for z in range(4)]
SPACE_PLANE = [[z * 8 + r for r in range(8)] for z in range(4)]
SPACE_Z = [[z * 8 + r for z in range(4)] for r in range(8)]


def copies(x, axis, groups):
    count = len(groups[0])
    sent = jnp.broadcast_to(x[None], (count,) + x.shape)
    return lax.all_to_all(sent, axis, 0, 0, axis_index_groups=groups)


def space_sum(x, beside=None):
    near = jnp.sum(copies(x, "space", SPACE_PLANE), axis=0)
    near, beside = lax.optimization_barrier((near, beside))
    return lax.psum(near, "space", axis_index_groups=SPACE_Z), beside


def products(vectors, states):
    return jnp.einsum(
        "vc,jc->vj",
        vectors,
        states,
        precision=lax.Precision.HIGH,
        preferred_element_type=jnp.float32,
    )


def combination(margin, states):
    return jnp.einsum(
        "vj,jc->vc",
        margin,
        states,
        precision=lax.Precision.HIGH,
        preferred_element_type=jnp.float32,
    )


def neighbours(vectors):
    count = lax.axis_size("space")
    outer = [(i, i + 1) for i in range(1, count - 1, 2)]
    outer = outer + [(j, i) for i, j in outer]
    across = lax.ppermute(vectors, "space", outer)
    inside = lax.ppermute(vectors, "space", [(i, i ^ 1) for i in range(count)])
    first = lax.axis_index("space") % 2 == 0
    return jnp.where(first, across, inside), jnp.where(first, inside, across)


def shifted(planes, by):
    length = planes.shape[-1]
    pad = [(0, 0)] * (planes.ndim - 1)
    if by > 0:
        return jnp.pad(planes[..., by:], pad + [(0, by)])
    return jnp.pad(planes[..., :length + by], pad + [(-by, 0)])


def coupling(vectors, low, high):
    z = jnp.arange(vectors.shape[-1]) % NZ
    nearest = shifted(vectors, NZ) + shifted(vectors, -NZ)
    second = shifted(vectors, 2 * NZ) + shifted(vectors, -2 * NZ)
    nearest = nearest + jnp.where(z >= 1, shifted(vectors, -1), 0.0)
    nearest = nearest + jnp.where(z <= NZ - 2, shifted(vectors, 1), 0.0)
    second = second + jnp.where(z >= 2, shifted(vectors, -2), 0.0)
    second = second + jnp.where(z <= NZ - 3, shifted(vectors, 2), 0.0)
    x = jnp.concatenate([low, vectors, high], axis=1)
    nearest = nearest + x[:, 1:3] + x[:, 3:5]
    second = second + x[:, 0:2] + x[:, 4:6]
    return second / 24.0 - 2.0 / 3.0 * nearest


def swapped(x, bit):
    return lax.ppermute(x, "band", [(i, i ^ bit) for i in range(lax.axis_size("band"))])


def shared_margin(halves, pair, weight, beside=None):
    product = jnp.concatenate([products(pair, half) for half in halves], axis=1)
    total, beside = space_sum(product, beside)
    return total * weight, beside


def shared_correction(margin, halves):
    width = halves[0].shape[0]
    return combination(margin[:, :width], halves[0]) + combination(margin[:, width:], halves[1])


def project_whole(states, vectors, weight):
    margin = space_sum(products(vectors, states))[0] * weight
    return vectors - combination(margin, states)


def on_device(occupied, initial, right_side, potential, energies):
    count, planes, line = initial.shape
    cells = planes * line
    weight = 1.0 / (lax.axis_size("space") * cells)
    blocks, own = occupied.shape[:2]
    states = occupied.reshape(blocks, own, cells)
    column = lax.all_gather(states, "band", axis=1, tiled=True, axis_index_groups=BAND_Z)
    ring = copies(states, "band", BAND_Y)
    first, second = ring[:, 0].reshape(-1, cells), ring[:, 1].reshape(-1, cells)
    diagonal = 3.75 + potential[None, :, :] - energies[:, None, None]
    vectors = initial.reshape(count, cells)
    pair = jnp.concatenate([vectors, swapped(vectors, 8)], axis=0)
    across_first, second = lax.optimization_barrier((swapped(first, 4), second))
    across_second = swapped(second, 4)
    halves = (first, across_first)
    margin, column = shared_margin(halves, pair, weight, column)
    whole = lax.all_gather(column, "band", axis=1, tiled=True, axis_index_groups=BAND_Y)
    partial = shared_correction(margin, halves)
    other = swapped(jnp.concatenate([partial[count:], partial[:count]], axis=0), 8)
    pair = pair - partial - other
    halves = (second, across_second)
    margin, _ = shared_margin(halves, pair, weight)
    partial = shared_correction(margin, halves)
    vectors = pair[:count] - partial[:count] - swapped(partial[count:], 8)
    vectors, whole = lax.optimization_barrier((vectors, whole))
    blocks = [lax.optimization_barrier(whole[block]) for block in range(2)]
    for iteration in range(ITERS):
        if iteration > 0:
            for block in blocks:
                vectors = project_whole(block, vectors, weight)
        low, high = neighbours(vectors)
        shape = (count, planes, line)
        vectors = vectors.reshape(shape)
        rest = right_side - coupling(vectors, low.reshape(shape), high.reshape(shape))
        residual = rest - diagonal * vectors
        vectors = (rest / diagonal).reshape(count, cells)
    return (vectors.reshape(shape), residual)


def solution(mesh):
    return jax.shard_map(
        on_device,
        mesh=mesh,
        in_specs=(
            P(None, "band", "space", None),
            P("band", "space", None),
            P("band", "space", None),
            P("space", None),
            P("band"),
        ),
        out_specs=(P("band", "space", None), P("band", "space", None)),
        check_vma=False,
    )
```

```python
import jax
import jax.numpy as jnp
from jax import lax
from jax.sharding import PartitionSpec as P

NZ = 32
ITERS = 2
BAND_Z = [[z * 4 + y for z in range(4)] for y in range(4)]
BAND_Y = [[z * 4 + y for y in range(4)] for z in range(4)]
SPACE_PLANE = [[z * 8 + r for r in range(8)] for z in range(4)]
SPACE_Z = [[z * 8 + r for z in range(4)] for r in range(8)]


def copies(x, axis, groups):
    count = len(groups[0])
    sent = jnp.broadcast_to(x[None], (count,) + x.shape)
    return lax.all_to_all(sent, axis, 0, 0, axis_index_groups=groups)


def space_sum(x, beside=None):
    near = jnp.sum(copies(x, "space", SPACE_PLANE), axis=0)
    near, beside = lax.optimization_barrier((near, beside))
    return lax.psum(near, "space", axis_index_groups=SPACE_Z), beside


def products(vectors, states):
    return jnp.einsum(
        "vc,jc->vj",
        vectors,
        states,
        precision=lax.Precision.HIGH,
        preferred_element_type=jnp.float32,
    )


def combination(margin, states):
    return jnp.einsum(
        "vj,jc->vc",
        margin,
        states,
        precision=lax.Precision.HIGH,
        preferred_element_type=jnp.float32,
    )


def neighbours(vectors):
    count = lax.axis_size("space")
    outer = [(i, i + 1) for i in range(1, count - 1, 2)]
    outer = outer + [(j, i) for i, j in outer]
    across = lax.ppermute(vectors, "space", outer)
    inside = lax.ppermute(vectors, "space", [(i, i ^ 1) for i in range(count)])
    first = lax.axis_index("space") % 2 == 0
    return jnp.where(first, across, inside), jnp.where(first, inside, across)


def shifted(planes, by):
    length = planes.shape[-1]
    pad = [(0, 0)] * (planes.ndim - 1)
    if by > 0:
        return jnp.pad(planes[..., by:], pad + [(0, by)])
    return jnp.pad(planes[..., :length + by], pad + [(-by, 0)])


def coupling(vectors, low, high):
    z = jnp.arange(vectors.shape[-1]) % NZ
    nearest = shifted(vectors, NZ) + shifted(vectors, -NZ)
    second = shifted(vectors, 2 * NZ) + shifted(vectors, -2 * NZ)
    nearest = nearest + jnp.where(z >= 1, shifted(vectors, -1), 0.0)
    nearest = nearest + jnp.where(z <= NZ - 2, shifted(vectors, 1), 0.0)
    second = second + jnp.where(z >= 2, shifted(vectors, -2), 0.0)
    second = second + jnp.where(z <= NZ - 3, shifted(vectors, 2), 0.0)
    x = jnp.concatenate([low, vectors, high], axis=1)
    nearest = nearest + x[:, 1:3] + x[:, 3:5]
    second = second + x[:, 0:2] + x[:, 4:6]
    return second / 24.0 - 2.0 / 3.0 * nearest


def swapped(x, bit):
    return lax.ppermute(x, "band", [(i, i ^ bit) for i in range(lax.axis_size("band"))])


def shared_margin(halves, pair, weight, beside=None):
    product = jnp.concatenate([products(pair, half) for half in halves], axis=1)
    total, beside = space_sum(product, beside)
    return total * weight, beside


def shared_correction(margin, halves):
    width = halves[0].shape[0]
    return combination(margin[:, :width], halves[0]) + combination(margin[:, width:], halves[1])


def project_whole(parts, vectors, weight):
    product = jnp.concatenate([products(vectors, part) for part in parts], axis=1)
    margin = space_sum(product)[0] * weight
    at = 0
    for part in parts:
        vectors = vectors - combination(margin[:, at : at + part.shape[0]], part)
        at += part.shape[0]
    return vectors


def on_device(occupied, initial, right_side, potential, energies):
    count, planes, line = initial.shape
    cells = planes * line
    weight = 1.0 / (lax.axis_size("space") * cells)
    blocks, own = occupied.shape[:2]
    states = occupied.reshape(blocks, own, cells)
    far = (swapped(states, 8), swapped(states, 12))
    ring = copies(states, "band", BAND_Y)
    first, second = ring[:, 0].reshape(-1, cells), ring[:, 1].reshape(-1, cells)
    diagonal = 3.75 + potential[None, :, :] - energies[:, None, None]
    vectors = initial.reshape(count, cells)
    pair = jnp.concatenate([vectors, swapped(vectors, 8)], axis=0)
    across_first, second = lax.optimization_barrier((swapped(first, 4), second))
    across_second = swapped(second, 4)
    halves = (first, across_first)
    near = halves
    margin, (far, across_second) = shared_margin(halves, pair, weight, (far, across_second))
    far = lax.all_gather(
        jnp.concatenate(far, axis=1), "band", axis=1, tiled=True, axis_index_groups=BAND_Y
    )
    partial = shared_correction(margin, halves)
    other = swapped(jnp.concatenate([partial[count:], partial[:count]], axis=0), 8)
    pair = pair - partial - other
    halves = (second, across_second)
    margin, _ = shared_margin(halves, pair, weight)
    partial = shared_correction(margin, halves)
    vectors = pair[:count] - partial[:count] - swapped(partial[count:], 8)
    vectors, far = lax.optimization_barrier((vectors, far))
    blocks = [near + (lax.optimization_barrier(far[0]),), halves + (lax.optimization_barrier(far[1]),)]
    for iteration in range(ITERS):
        if iteration > 0:
            for block in blocks:
                vectors = project_whole(block, vectors, weight)
        low, high = neighbours(vectors)
        shape = (count, planes, line)
        vectors = vectors.reshape(shape)
        rest = right_side - coupling(vectors, low.reshape(shape), high.reshape(shape))
        residual = rest - diagonal * vectors
        vectors = (rest / diagonal).reshape(count, cells)
    return (vectors.reshape(shape), residual)


def solution(mesh):
    return jax.shard_map(
        on_device,
        mesh=mesh,
        in_specs=(
            P(None, "band", "space", None),
            P("band", "space", None),
            P("band", "space", None),
            P("space", None),
            P("band"),
        ),
        out_specs=(P("band", "space", None), P("band", "space", None)),
        check_vma=False,
    )
```

```python
import jax
import jax.numpy as jnp
from jax import lax
from jax.sharding import PartitionSpec as P

NZ = 32
ITERS = 2
BAND_Z = [[z * 4 + y for z in range(4)] for y in range(4)]
BAND_Y = [[z * 4 + y for y in range(4)] for z in range(4)]
SPACE_PLANE = [[z * 8 + r for r in range(8)] for z in range(4)]
SPACE_Z = [[z * 8 + r for z in range(4)] for r in range(8)]


def copies(x, axis, groups):
    count = len(groups[0])
    sent = jnp.broadcast_to(x[None], (count,) + x.shape)
    return lax.all_to_all(sent, axis, 0, 0, axis_index_groups=groups)


def space_sum(x):
    near = jnp.sum(copies(x, "space", SPACE_PLANE), axis=0)
    return lax.psum(near, "space", axis_index_groups=SPACE_Z)


def products(vectors, states):
    return jnp.einsum(
        "vc,jc->vj",
        vectors,
        states,
        precision=lax.Precision.HIGH,
        preferred_element_type=jnp.float32,
    )


def combination(margin, states):
    return jnp.einsum(
        "vj,jc->vc",
        margin,
        states,
        precision=lax.Precision.HIGH,
        preferred_element_type=jnp.float32,
    )


def neighbours(vectors):
    count = lax.axis_size("space")
    outer = [(i, i + 1) for i in range(1, count - 1, 2)]
    outer = outer + [(j, i) for i, j in outer]
    across = lax.ppermute(vectors, "space", outer)
    inside = lax.ppermute(vectors, "space", [(i, i ^ 1) for i in range(count)])
    first = lax.axis_index("space") % 2 == 0
    return jnp.where(first, across, inside), jnp.where(first, inside, across)


def shifted(planes, by):
    length = planes.shape[-1]
    pad = [(0, 0)] * (planes.ndim - 1)
    if by > 0:
        return jnp.pad(planes[..., by:], pad + [(0, by)])
    return jnp.pad(planes[..., :length + by], pad + [(-by, 0)])


def coupling(vectors, low, high):
    z = jnp.arange(vectors.shape[-1]) % NZ
    nearest = shifted(vectors, NZ) + shifted(vectors, -NZ)
    second = shifted(vectors, 2 * NZ) + shifted(vectors, -2 * NZ)
    nearest = nearest + jnp.where(z >= 1, shifted(vectors, -1), 0.0)
    nearest = nearest + jnp.where(z <= NZ - 2, shifted(vectors, 1), 0.0)
    second = second + jnp.where(z >= 2, shifted(vectors, -2), 0.0)
    second = second + jnp.where(z <= NZ - 3, shifted(vectors, 2), 0.0)
    x = jnp.concatenate([low, vectors, high], axis=1)
    nearest = nearest + x[:, 1:3] + x[:, 3:5]
    second = second + x[:, 0:2] + x[:, 4:6]
    return second / 24.0 - 2.0 / 3.0 * nearest


def swapped(x, bit):
    return lax.ppermute(x, "band", [(i, i ^ bit) for i in range(lax.axis_size("band"))])


def shared_margin(halves, pair, weight):
    product = jnp.concatenate([products(pair, half) for half in halves], axis=1)
    return space_sum(product) * weight


def shared_correction(margin, halves):
    width = halves[0].shape[0]
    return combination(margin[:, :width], halves[0]) + combination(margin[:, width:], halves[1])


def project_whole(parts, vectors, weight):
    product = jnp.concatenate([products(vectors, part) for part in parts], axis=1)
    margin = space_sum(product) * weight
    at = 0
    for part in parts:
        vectors = vectors - combination(margin[:, at : at + part.shape[0]], part)
        at += part.shape[0]
    return vectors


def on_device(occupied, initial, right_side, potential, energies):
    count, planes, line = initial.shape
    cells = planes * line
    weight = 1.0 / (lax.axis_size("space") * cells)
    blocks, own = occupied.shape[:2]
    states = occupied.reshape(blocks, own, cells)
    ring = copies(states, "band", BAND_Y)
    first, second = ring[:, 0].reshape(-1, cells), ring[:, 1].reshape(-1, cells)
    diagonal = 3.75 + potential[None, :, :] - energies[:, None, None]
    vectors = initial.reshape(count, cells)
    pair = jnp.concatenate([vectors, swapped(vectors, 8)], axis=0)
    across_first, second, states = lax.optimization_barrier((swapped(first, 4), second, states))
    across_second = swapped(second, 4)
    far = (swapped(states, 8), swapped(states, 12))
    halves = (first, across_first)
    near = halves
    margin = shared_margin(halves, pair, weight)
    margin, far, across_second = lax.optimization_barrier((margin, far, across_second))
    far = lax.all_gather(
        jnp.concatenate(far, axis=1), "band", axis=1, tiled=True, axis_index_groups=BAND_Y
    )
    partial = shared_correction(margin, halves)
    other = swapped(jnp.concatenate([partial[count:], partial[:count]], axis=0), 8)
    pair = pair - partial - other
    halves = (second, across_second)
    margin = shared_margin(halves, pair, weight)
    partial = shared_correction(margin, halves)
    vectors = pair[:count] - partial[:count] - swapped(partial[count:], 8)
    vectors, far = lax.optimization_barrier((vectors, far))
    blocks = [near + (lax.optimization_barrier(far[0]),), halves + (lax.optimization_barrier(far[1]),)]
    for iteration in range(ITERS):
        if iteration > 0:
            for block in blocks:
                vectors = project_whole(block, vectors, weight)
        low, high = neighbours(vectors)
        shape = (count, planes, line)
        vectors = vectors.reshape(shape)
        rest = right_side - coupling(vectors, low.reshape(shape), high.reshape(shape))
        residual = rest - diagonal * vectors
        vectors = (rest / diagonal).reshape(count, cells)
    return (vectors.reshape(shape), residual)


def solution(mesh):
    return jax.shard_map(
        on_device,
        mesh=mesh,
        in_specs=(
            P(None, "band", "space", None),
            P("band", "space", None),
            P("band", "space", None),
            P("space", None),
            P("band"),
        ),
        out_specs=(P("band", "space", None), P("band", "space", None)),
        check_vma=False,
    )
```

```python
import jax
import jax.numpy as jnp
from jax import lax
from jax.sharding import PartitionSpec as P

NZ = 32
ITERS = 2
BAND_Z = [[z * 4 + y for z in range(4)] for y in range(4)]
BAND_Y = [[z * 4 + y for y in range(4)] for z in range(4)]
SPACE_PLANE = [[z * 8 + r for r in range(8)] for z in range(4)]
SPACE_Z = [[z * 8 + r for z in range(4)] for r in range(8)]


def copies(x, axis, groups):
    count = len(groups[0])
    sent = jnp.broadcast_to(x[None], (count,) + x.shape)
    return lax.all_to_all(sent, axis, 0, 0, axis_index_groups=groups)


def space_sum(x):
    near = jnp.sum(copies(x, "space", SPACE_PLANE), axis=0)
    return lax.psum(near, "space", axis_index_groups=SPACE_Z)


def products(vectors, states):
    return jnp.einsum(
        "vc,jc->vj",
        vectors,
        states,
        precision=lax.Precision.HIGH,
        preferred_element_type=jnp.float32,
    )


def combination(margin, states):
    return jnp.einsum(
        "vj,jc->vc",
        margin,
        states,
        precision=lax.Precision.HIGH,
        preferred_element_type=jnp.float32,
    )


def neighbours(vectors):
    count = lax.axis_size("space")
    outer = [(i, i + 1) for i in range(1, count - 1, 2)]
    outer = outer + [(j, i) for i, j in outer]
    across = lax.ppermute(vectors, "space", outer)
    inside = lax.ppermute(vectors, "space", [(i, i ^ 1) for i in range(count)])
    first = lax.axis_index("space") % 2 == 0
    return jnp.where(first, across, inside), jnp.where(first, inside, across)


def shifted(planes, by):
    length = planes.shape[-1]
    pad = [(0, 0)] * (planes.ndim - 1)
    if by > 0:
        return jnp.pad(planes[..., by:], pad + [(0, by)])
    return jnp.pad(planes[..., :length + by], pad + [(-by, 0)])


def coupling(vectors, low, high):
    z = jnp.arange(vectors.shape[-1]) % NZ
    nearest = shifted(vectors, NZ) + shifted(vectors, -NZ)
    second = shifted(vectors, 2 * NZ) + shifted(vectors, -2 * NZ)
    nearest = nearest + jnp.where(z >= 1, shifted(vectors, -1), 0.0)
    nearest = nearest + jnp.where(z <= NZ - 2, shifted(vectors, 1), 0.0)
    second = second + jnp.where(z >= 2, shifted(vectors, -2), 0.0)
    second = second + jnp.where(z <= NZ - 3, shifted(vectors, 2), 0.0)
    x = jnp.concatenate([low, vectors, high], axis=1)
    nearest = nearest + x[:, 1:3] + x[:, 3:5]
    second = second + x[:, 0:2] + x[:, 4:6]
    return second / 24.0 - 2.0 / 3.0 * nearest


def swapped(x, bit):
    return lax.ppermute(x, "band", [(i, i ^ bit) for i in range(lax.axis_size("band"))])


def shared_margin(halves, pair, weight):
    product = jnp.concatenate([products(pair, half) for half in halves], axis=1)
    return space_sum(product) * weight


def shared_correction(margin, halves):
    width = halves[0].shape[0]
    return combination(margin[:, :width], halves[0]) + combination(margin[:, width:], halves[1])


def project_whole(parts, vectors, weight):
    product = jnp.concatenate([products(vectors, part) for part in parts], axis=1)
    margin = space_sum(product) * weight
    at = 0
    for part in parts:
        vectors = vectors - combination(margin[:, at : at + part.shape[0]], part)
        at += part.shape[0]
    return vectors


def on_device(occupied, initial, right_side, potential, energies):
    count, planes, line = initial.shape
    cells = planes * line
    weight = 1.0 / (lax.axis_size("space") * cells)
    blocks, own = occupied.shape[:2]
    states = occupied.reshape(blocks, own, cells)
    column = lax.all_gather(states, "band", axis=1, tiled=True, axis_index_groups=BAND_Z)
    ring = copies(states, "band", BAND_Y)
    first, second = ring[:, 0].reshape(-1, cells), ring[:, 1].reshape(-1, cells)
    diagonal = 3.75 + potential[None, :, :] - energies[:, None, None]
    vectors = initial.reshape(count, cells)
    pair = jnp.concatenate([vectors, swapped(vectors, 8)], axis=0)
    across_first, second = lax.optimization_barrier((swapped(first, 4), second))
    across_second = swapped(second, 4)
    halves = (first, across_first)
    near = halves
    margin = shared_margin(halves, pair, weight)
    margin, column = lax.optimization_barrier((margin, column))
    upper = lax.axis_index("band") // 8
    far = lax.dynamic_slice_in_dim(column, (1 - upper) * 2 * own, 2 * own, axis=1)
    far = lax.all_gather(far, "band", axis=1, tiled=True, axis_index_groups=BAND_Y)
    partial = shared_correction(margin, halves)
    other = swapped(jnp.concatenate([partial[count:], partial[:count]], axis=0), 8)
    pair = pair - partial - other
    halves = (second, across_second)
    margin = shared_margin(halves, pair, weight)
    partial = shared_correction(margin, halves)
    vectors = pair[:count] - partial[:count] - swapped(partial[count:], 8)
    vectors, far = lax.optimization_barrier((vectors, far))
    blocks = [near + (lax.optimization_barrier(far[0]),), halves + (lax.optimization_barrier(far[1]),)]
    for iteration in range(ITERS):
        if iteration > 0:
            for block in blocks:
                vectors = project_whole(block, vectors, weight)
        low, high = neighbours(vectors)
        shape = (count, planes, line)
        vectors = vectors.reshape(shape)
        rest = right_side - coupling(vectors, low.reshape(shape), high.reshape(shape))
        residual = rest - diagonal * vectors
        vectors = (rest / diagonal).reshape(count, cells)
    return (vectors.reshape(shape), residual)


def solution(mesh):
    return jax.shard_map(
        on_device,
        mesh=mesh,
        in_specs=(
            P(None, "band", "space", None),
            P("band", "space", None),
            P("band", "space", None),
            P("space", None),
            P("band"),
        ),
        out_specs=(P("band", "space", None), P("band", "space", None)),
        check_vma=False,
    )
```

```python
import jax
import jax.numpy as jnp
from jax import lax
from jax.sharding import PartitionSpec as P

NZ = 32
ITERS = 2
BAND_Z = [[z * 4 + y for z in range(4)] for y in range(4)]
SPACE_PLANE = [[z * 8 + r for r in range(8)] for z in range(4)]
SPACE_Z = [[z * 8 + r for z in range(4)] for r in range(8)]


def copies(x, axis, groups):
    count = len(groups[0])
    sent = jnp.broadcast_to(x[None], (count,) + x.shape)
    return lax.all_to_all(sent, axis, 0, 0, axis_index_groups=groups)


def space_sum(x):
    near = jnp.sum(copies(x, "space", SPACE_PLANE), axis=0)
    return lax.psum(near, "space", axis_index_groups=SPACE_Z)


def products(vectors, states):
    return jnp.einsum(
        "vc,jc->vj",
        vectors,
        states,
        precision=lax.Precision.HIGH,
        preferred_element_type=jnp.float32,
    )


def combination(margin, states):
    return jnp.einsum(
        "vj,jc->vc",
        margin,
        states,
        precision=lax.Precision.HIGH,
        preferred_element_type=jnp.float32,
    )


def neighbours(vectors):
    count = lax.axis_size("space")
    outer = [(i, i + 1) for i in range(1, count - 1, 2)]
    outer = outer + [(j, i) for i, j in outer]
    across = lax.ppermute(vectors, "space", outer)
    inside = lax.ppermute(vectors, "space", [(i, i ^ 1) for i in range(count)])
    first = lax.axis_index("space") % 2 == 0
    return jnp.where(first, across, inside), jnp.where(first, inside, across)


def shifted(planes, by):
    length = planes.shape[-1]
    pad = [(0, 0)] * (planes.ndim - 1)
    if by > 0:
        return jnp.pad(planes[..., by:], pad + [(0, by)])
    return jnp.pad(planes[..., :length + by], pad + [(-by, 0)])


def coupling(vectors, low, high):
    z = jnp.arange(vectors.shape[-1]) % NZ
    nearest = shifted(vectors, NZ) + shifted(vectors, -NZ)
    second = shifted(vectors, 2 * NZ) + shifted(vectors, -2 * NZ)
    nearest = nearest + jnp.where(z >= 1, shifted(vectors, -1), 0.0)
    nearest = nearest + jnp.where(z <= NZ - 2, shifted(vectors, 1), 0.0)
    second = second + jnp.where(z >= 2, shifted(vectors, -2), 0.0)
    second = second + jnp.where(z <= NZ - 3, shifted(vectors, 2), 0.0)
    x = jnp.concatenate([low, vectors, high], axis=1)
    nearest = nearest + x[:, 1:3] + x[:, 3:5]
    second = second + x[:, 0:2] + x[:, 4:6]
    return second / 24.0 - 2.0 / 3.0 * nearest


def swapped(x, bits):
    return lax.ppermute(x, "band", [(i, i ^ bits) for i in range(lax.axis_size("band"))])


def project_whole(parts, vectors, weight):
    product = jnp.concatenate([products(vectors, part) for part in parts], axis=1)
    margin = space_sum(product) * weight
    at = 0
    for part in parts:
        vectors = vectors - combination(margin[:, at : at + part.shape[0]], part)
        at += part.shape[0]
    return vectors


def on_device(occupied, initial, right_side, potential, energies):
    count, planes, line = initial.shape
    cells = planes * line
    weight = 1.0 / (lax.axis_size("space") * cells)
    tie = lax.optimization_barrier
    own = [states.reshape(-1, cells) for states in occupied]
    diagonal = 3.75 + potential[None, :, :] - energies[:, None, None]
    vectors = initial.reshape(count, cells)
    run, other = tie((copies(own[0], "band", BAND_Z).reshape(-1, cells), own[1]))
    across = swapped(run, 1)
    second = copies(other, "band", BAND_Z).reshape(-1, cells)
    pair = jnp.concatenate([vectors, swapped(vectors, 3)], axis=0)
    across, second, pair = tie((across, second, pair))
    near = [jnp.concatenate([run, across], axis=0)]
    margin = space_sum(products(pair, near[0])) * weight
    margin, across, far = tie((margin, swapped(second, 1), swapped(near[0], 3)))
    partial = combination(margin, near[0])
    other = swapped(jnp.concatenate([partial[count:], partial[:count]], axis=0), 3)
    pair, second, across = tie((pair - partial - other, second, across))
    near.append(jnp.concatenate([second, across], axis=0))
    margin = space_sum(products(pair, near[1])) * weight
    margin, far_second = tie((margin, swapped(near[1], 3)))
    partial = combination(margin, near[1])
    vectors = pair[:count] - partial[:count] - swapped(partial[count:], 3)
    blocks = [(near[0], far), (near[1], far_second)]
    for iteration in range(ITERS):
        if iteration > 0:
            for block in blocks:
                vectors = project_whole(block, vectors, weight)
        low, high = neighbours(vectors)
        shape = (count, planes, line)
        vectors = vectors.reshape(shape)
        rest = right_side - coupling(vectors, low.reshape(shape), high.reshape(shape))
        residual = rest - diagonal * vectors
        vectors = (rest / diagonal).reshape(count, cells)
    return (vectors.reshape(shape), residual)


def solution(mesh):
    return jax.shard_map(
        on_device,
        mesh=mesh,
        in_specs=(
            P(None, "band", "space", None),
            P("band", "space", None),
            P("band", "space", None),
            P("space", None),
            P("band"),
        ),
        out_specs=(P("band", "space", None), P("band", "space", None)),
        check_vma=False,
    )
```

```python
import jax
import jax.numpy as jnp
from jax import lax
from jax.sharding import PartitionSpec as P

NZ = 32
ITERS = 2
BAND_Z = [[z * 4 + y for z in range(4)] for y in range(4)]
SPACE_PLANE = [[z * 8 + r for r in range(8)] for z in range(4)]
SPACE_Z = [[z * 8 + r for z in range(4)] for r in range(8)]


def copies(x, axis, groups):
    count = len(groups[0])
    sent = jnp.broadcast_to(x[None], (count,) + x.shape)
    return lax.all_to_all(sent, axis, 0, 0, axis_index_groups=groups)


def space_sum(x):
    near = jnp.sum(copies(x, "space", SPACE_PLANE), axis=0)
    return lax.psum(near, "space", axis_index_groups=SPACE_Z)


def products(vectors, states):
    return jnp.einsum(
        "vc,jc->vj",
        vectors,
        states,
        precision=lax.Precision.HIGH,
        preferred_element_type=jnp.float32,
    )


def combination(margin, states):
    return jnp.einsum(
        "vj,jc->vc",
        margin,
        states,
        precision=lax.Precision.HIGH,
        preferred_element_type=jnp.float32,
    )


def neighbours(vectors):
    count = lax.axis_size("space")
    outer = [(i, i + 1) for i in range(1, count - 1, 2)]
    outer = outer + [(j, i) for i, j in outer]
    inside = lax.ppermute(vectors, "space", [(i, i ^ 1) for i in range(count)])
    across = lax.ppermute(vectors, "space", outer)
    first = lax.axis_index("space") % 2 == 0
    return jnp.where(first, across, inside), jnp.where(first, inside, across)


def shifted(planes, by):
    length = planes.shape[-1]
    pad = [(0, 0)] * (planes.ndim - 1)
    if by > 0:
        return jnp.pad(planes[..., by:], pad + [(0, by)])
    return jnp.pad(planes[..., :length + by], pad + [(-by, 0)])


def coupling(vectors, low, high):
    z = jnp.arange(vectors.shape[-1]) % NZ
    nearest = shifted(vectors, NZ) + shifted(vectors, -NZ)
    second = shifted(vectors, 2 * NZ) + shifted(vectors, -2 * NZ)
    nearest = nearest + jnp.where(z >= 1, shifted(vectors, -1), 0.0)
    nearest = nearest + jnp.where(z <= NZ - 2, shifted(vectors, 1), 0.0)
    second = second + jnp.where(z >= 2, shifted(vectors, -2), 0.0)
    second = second + jnp.where(z <= NZ - 3, shifted(vectors, 2), 0.0)
    x = jnp.concatenate([low, vectors, high], axis=1)
    nearest = nearest + x[:, 1:3] + x[:, 3:5]
    second = second + x[:, 0:2] + x[:, 4:6]
    return second / 24.0 - 2.0 / 3.0 * nearest


def swapped(x, bits):
    return lax.ppermute(x, "band", [(i, i ^ bits) for i in range(lax.axis_size("band"))])


def project_whole(parts, vectors, weight):
    product = jnp.concatenate([products(vectors, part) for part in parts], axis=1)
    margin = space_sum(product) * weight
    at = 0
    for part in parts:
        vectors = vectors - combination(margin[:, at : at + part.shape[0]], part)
        at += part.shape[0]
    return vectors


def on_device(occupied, initial, right_side, potential, energies):
    count, planes, line = initial.shape
    cells = planes * line
    weight = 1.0 / (lax.axis_size("space") * cells)
    tie = lax.optimization_barrier
    own = [states.reshape(-1, cells) for states in occupied]
    diagonal = 3.75 + potential[None, :, :] - energies[:, None, None]
    vectors = initial.reshape(count, cells)
    pair = jnp.concatenate([vectors, swapped(vectors, 3)], axis=0)
    run = copies(own[0], "band", BAND_Z).reshape(-1, cells)
    run, other, pair = tie((run, own[1], pair))
    across = swapped(run, 1)
    second = copies(other, "band", BAND_Z).reshape(-1, cells)
    across, second = tie((across, second))
    near = [jnp.concatenate([run, across], axis=0)]
    margin = space_sum(products(pair, near[0])) * weight
    margin, across, far = tie((margin, swapped(second, 1), swapped(near[0], 3)))
    partial = combination(margin, near[0])
    other = swapped(jnp.concatenate([partial[count:], partial[:count]], axis=0), 3)
    pair, second, across = tie((pair - partial - other, second, across))
    near.append(jnp.concatenate([second, across], axis=0))
    margin = space_sum(products(pair, near[1])) * weight
    partial = combination(margin, near[1])
    vectors = pair[:count] - partial[:count] - swapped(partial[count:], 3)
    vectors, sent = tie((vectors, near[1]))
    blocks = [(near[0], far), (near[1], swapped(sent, 3))]
    for iteration in range(ITERS):
        if iteration > 0:
            for block in blocks:
                vectors = project_whole(block, vectors, weight)
        low, high = neighbours(vectors)
        shape = (count, planes, line)
        vectors = vectors.reshape(shape)
        rest = right_side - coupling(vectors, low.reshape(shape), high.reshape(shape))
        residual = rest - diagonal * vectors
        vectors = (rest / diagonal).reshape(count, cells)
    return (vectors.reshape(shape), residual)


def solution(mesh):
    return jax.shard_map(
        on_device,
        mesh=mesh,
        in_specs=(
            P(None, "band", "space", None),
            P("band", "space", None),
            P("band", "space", None),
            P("space", None),
            P("band"),
        ),
        out_specs=(P("band", "space", None), P("band", "space", None)),
        check_vma=False,
    )
```

```python
import jax
import jax.numpy as jnp
from jax import lax
from jax.sharding import PartitionSpec as P

NZ = 32
ITERS = 2
BAND_Z = [[z * 4 + y for z in range(4)] for y in range(4)]
BAND_Y = [[z * 4 + y for y in range(4)] for z in range(4)]
SPACE_PLANE = [[z * 8 + r for r in range(8)] for z in range(4)]
SPACE_Z = [[z * 8 + r for z in range(4)] for r in range(8)]


def copies(x, axis, groups):
    count = len(groups[0])
    sent = jnp.broadcast_to(x[None], (count,) + x.shape)
    return lax.all_to_all(sent, axis, 0, 0, axis_index_groups=groups)


def space_sum(x):
    near = jnp.sum(copies(x, "space", SPACE_PLANE), axis=0)
    return lax.psum(near, "space", axis_index_groups=SPACE_Z)


def products(vectors, states):
    return jnp.einsum(
        "vc,jc->vj",
        vectors,
        states,
        precision=lax.Precision.HIGH,
        preferred_element_type=jnp.float32,
    )


def combination(margin, states):
    return jnp.einsum(
        "vj,jc->vc",
        margin,
        states,
        precision=lax.Precision.HIGH,
        preferred_element_type=jnp.float32,
    )


def summed_margin(parts, vectors, weight):
    product = jnp.concatenate([products(vectors, part) for part in parts], axis=1)
    return space_sum(product) * weight


def corrected(parts, vectors, margin):
    at = 0
    for part in parts:
        vectors = vectors - combination(margin[:, at : at + part.shape[0]], part)
        at += part.shape[0]
    return vectors


def neighbours(vectors):
    count = lax.axis_size("space")
    outer = [(i, i + 1) for i in range(1, count - 1, 2)]
    outer = outer + [(j, i) for i, j in outer]
    inside = lax.ppermute(vectors, "space", [(i, i ^ 1) for i in range(count)])
    across = lax.ppermute(vectors, "space", outer)
    first = lax.axis_index("space") % 2 == 0
    return jnp.where(first, across, inside), jnp.where(first, inside, across)


def shifted(planes, by):
    length = planes.shape[-1]
    pad = [(0, 0)] * (planes.ndim - 1)
    if by > 0:
        return jnp.pad(planes[..., by:], pad + [(0, by)])
    return jnp.pad(planes[..., :length + by], pad + [(-by, 0)])


def coupling(vectors, low, high):
    z = jnp.arange(vectors.shape[-1]) % NZ
    nearest = shifted(vectors, NZ) + shifted(vectors, -NZ)
    second = shifted(vectors, 2 * NZ) + shifted(vectors, -2 * NZ)
    nearest = nearest + jnp.where(z >= 1, shifted(vectors, -1), 0.0)
    nearest = nearest + jnp.where(z <= NZ - 2, shifted(vectors, 1), 0.0)
    second = second + jnp.where(z >= 2, shifted(vectors, -2), 0.0)
    second = second + jnp.where(z <= NZ - 3, shifted(vectors, 2), 0.0)
    x = jnp.concatenate([low, vectors, high], axis=1)
    nearest = nearest + x[:, 1:3] + x[:, 3:5]
    second = second + x[:, 0:2] + x[:, 4:6]
    return second / 24.0 - 2.0 / 3.0 * nearest


def swapped(x, bits):
    return lax.ppermute(x, "band", [(i, i ^ bits) for i in range(lax.axis_size("band"))])


def on_device(occupied, initial, right_side, potential, energies):
    count, planes, line = initial.shape
    cells = planes * line
    weight = 1.0 / (lax.axis_size("space") * cells)
    tie = lax.optimization_barrier
    own = [states.reshape(-1, cells) for states in occupied]
    diagonal = 3.75 + potential[None, :, :] - energies[:, None, None]
    vectors = initial.reshape(count, cells)
    run = copies(jnp.stack(own), "band", BAND_Z)
    first, run = tie((copies(run[:, 0].reshape(-1, cells), "band", BAND_Y).reshape(-1, cells), run[:, 1]))
    run = run.reshape(-1, cells)
    second = (run,) + tuple(swapped(run, bits) for bits in (1, 3, 2))
    blocks = [(first,), second]
    for iteration in range(ITERS):
        for index in range(2):
            margin = summed_margin(blocks[index], vectors, weight)
            if iteration == 0 and index == 0:
                margin, blocks[1] = tie((margin, blocks[1]))
            vectors = corrected(blocks[index], vectors, margin)
        low, high = neighbours(vectors)
        shape = (count, planes, line)
        vectors = vectors.reshape(shape)
        rest = right_side - coupling(vectors, low.reshape(shape), high.reshape(shape))
        residual = rest - diagonal * vectors
        vectors = (rest / diagonal).reshape(count, cells)
    return (vectors.reshape(shape), residual)


def solution(mesh):
    return jax.shard_map(
        on_device,
        mesh=mesh,
        in_specs=(
            P(None, "band", "space", None),
            P("band", "space", None),
            P("band", "space", None),
            P("space", None),
            P("band"),
        ),
        out_specs=(P("band", "space", None), P("band", "space", None)),
        check_vma=False,
    )
```

```python
import jax
import jax.numpy as jnp
from jax import lax
from jax.sharding import PartitionSpec as P

NZ = 32
ITERS = 2
BAND_Z = [[z * 4 + y for z in range(4)] for y in range(4)]
PAIR_PLANE = [
    [(z * 4 + y) * 32 + far * 8 + r for y in pair for r in range(8)]
    for z in range(4)
    for pair in ((0, 3), (1, 2))
    for far in range(4)
]
SPACE_PLANE = [[z * 8 + r for r in range(8)] for z in range(4)]
SPACE_Z = [[z * 8 + r for z in range(4)] for r in range(8)]


def copies(x, axis, groups):
    count = len(groups[0])
    sent = jnp.broadcast_to(x[None], (count,) + x.shape)
    return lax.all_to_all(sent, axis, 0, 0, axis_index_groups=groups)


def space_sum(x):
    near = jnp.sum(copies(x, "space", SPACE_PLANE), axis=0)
    return lax.psum(near, "space", axis_index_groups=SPACE_Z)


def products(vectors, states):
    return jnp.einsum(
        "vc,jc->vj",
        vectors,
        states,
        precision=lax.Precision.HIGH,
        preferred_element_type=jnp.float32,
    )


def combination(margin, states):
    return jnp.einsum(
        "vj,jc->vc",
        margin,
        states,
        precision=lax.Precision.HIGH,
        preferred_element_type=jnp.float32,
    )


def neighbours(vectors):
    count = lax.axis_size("space")
    outer = [(i, i + 1) for i in range(1, count - 1, 2)]
    outer = outer + [(j, i) for i, j in outer]
    inside = lax.ppermute(vectors, "space", [(i, i ^ 1) for i in range(count)])
    across = lax.ppermute(vectors, "space", outer)
    first = lax.axis_index("space") % 2 == 0
    return jnp.where(first, across, inside), jnp.where(first, inside, across)


def shifted(planes, by):
    length = planes.shape[-1]
    pad = [(0, 0)] * (planes.ndim - 1)
    if by > 0:
        return jnp.pad(planes[..., by:], pad + [(0, by)])
    return jnp.pad(planes[..., :length + by], pad + [(-by, 0)])


def coupling(vectors, low, high):
    z = jnp.arange(vectors.shape[-1]) % NZ
    nearest = shifted(vectors, NZ) + shifted(vectors, -NZ)
    second = shifted(vectors, 2 * NZ) + shifted(vectors, -2 * NZ)
    nearest = nearest + jnp.where(z >= 1, shifted(vectors, -1), 0.0)
    nearest = nearest + jnp.where(z <= NZ - 2, shifted(vectors, 1), 0.0)
    second = second + jnp.where(z >= 2, shifted(vectors, -2), 0.0)
    second = second + jnp.where(z <= NZ - 3, shifted(vectors, 2), 0.0)
    x = jnp.concatenate([low, vectors, high], axis=1)
    nearest = nearest + x[:, 1:3] + x[:, 3:5]
    second = second + x[:, 0:2] + x[:, 4:6]
    return second / 24.0 - 2.0 / 3.0 * nearest


def swapped(x, bits):
    return lax.ppermute(x, "band", [(i, i ^ bits) for i in range(lax.axis_size("band"))])


def pair_margins(product, lower, weight):
    total = lax.psum(product, "space", axis_index_groups=SPACE_Z)
    every = weight * copies(total, ("band", "space"), PAIR_PLANE)
    ahead, behind = jnp.sum(every[:8], axis=0), jnp.sum(every[8:], axis=0)
    return jnp.where(lower, ahead, behind), jnp.where(lower, behind, ahead)


def project_whole(parts, vectors, weight):
    product = jnp.concatenate([products(vectors, part) for part in parts], axis=1)
    margin = space_sum(product) * weight
    at = 0
    for part in parts:
        vectors = vectors - combination(margin[:, at : at + part.shape[0]], part)
        at += part.shape[0]
    return vectors


def on_device(occupied, initial, right_side, potential, energies):
    count, planes, line = initial.shape
    cells = planes * line
    weight = 1.0 / (lax.axis_size("space") * cells)
    tie = lax.optimization_barrier
    own = [states.reshape(-1, cells) for states in occupied]
    diagonal = 3.75 + potential[None, :, :] - energies[:, None, None]
    vectors = initial.reshape(count, cells)
    lower = lax.axis_index("band") % 4 < 2
    partner = swapped(vectors, 3)
    pair = jnp.concatenate(
        [jnp.where(lower, vectors, partner), jnp.where(lower, partner, vectors)], axis=0
    )
    run = copies(own[0], "band", BAND_Z).reshape(-1, cells)
    run, other, pair = tie((run, own[1], pair))
    across = swapped(run, 1)
    second = copies(other, "band", BAND_Z).reshape(-1, cells)
    across, second = tie((across, second))
    near = jnp.concatenate([run, across], axis=0)
    margins = pair_margins(products(pair, near), lower, weight)
    margins, across, far = tie((margins, swapped(second, 1), swapped(near, 3)))
    first = (near, far)
    for margin, part in zip(margins, first):
        pair = pair - combination(margin, part)
    near = jnp.concatenate([second, across], axis=0)
    margins = pair_margins(products(pair, near), lower, weight)
    margins, far = tie((margins, swapped(near, 3)))
    blocks = [first, (near, far)]
    vectors = jnp.where(lower, pair[:count], pair[count:])
    for margin, part in zip(margins, blocks[1]):
        vectors = vectors - combination(jnp.where(lower, margin[:count], margin[count:]), part)
    for iteration in range(ITERS):
        if iteration > 0:
            for block in blocks:
                vectors = project_whole(block, vectors, weight)
        low, high = neighbours(vectors)
        shape = (count, planes, line)
        vectors = vectors.reshape(shape)
        rest = right_side - coupling(vectors, low.reshape(shape), high.reshape(shape))
        residual = rest - diagonal * vectors
        vectors = (rest / diagonal).reshape(count, cells)
    return (vectors.reshape(shape), residual)


def solution(mesh):
    return jax.shard_map(
        on_device,
        mesh=mesh,
        in_specs=(
            P(None, "band", "space", None),
            P("band", "space", None),
            P("band", "space", None),
            P("space", None),
            P("band"),
        ),
        out_specs=(P("band", "space", None), P("band", "space", None)),
        check_vma=False,
    )
```

```python
import jax
import jax.numpy as jnp
from jax import lax
from jax.sharding import PartitionSpec as P

NZ = 32
ITERS = 2
BAND_Z = [[z * 4 + y for z in range(4)] for y in range(4)]
PAIR_PLANE = [
    [(z * 4 + y) * 32 + far * 8 + r for y in pair for r in range(8)]
    for z in range(4)
    for pair in ((0, 3), (1, 2))
    for far in range(4)
]
SPACE_PLANE = [[z * 8 + r for r in range(8)] for z in range(4)]
SPACE_Z = [[z * 8 + r for z in range(4)] for r in range(8)]


def copies(x, axis, groups):
    count = len(groups[0])
    sent = jnp.broadcast_to(x[None], (count,) + x.shape)
    return lax.all_to_all(sent, axis, 0, 0, axis_index_groups=groups)


def space_sum(x):
    near = jnp.sum(copies(x, "space", SPACE_PLANE), axis=0)
    return lax.psum(near, "space", axis_index_groups=SPACE_Z)


def products(vectors, states):
    return jnp.einsum(
        "vc,jc->vj",
        vectors,
        states,
        precision=lax.Precision.HIGH,
        preferred_element_type=jnp.float32,
    )


def combination(margin, states):
    return jnp.einsum(
        "vj,jc->vc",
        margin,
        states,
        precision=lax.Precision.HIGH,
        preferred_element_type=jnp.float32,
    )


def neighbours(vectors):
    count = lax.axis_size("space")
    outer = [(i, i + 1) for i in range(1, count - 1, 2)]
    outer = outer + [(j, i) for i, j in outer]
    inside = lax.ppermute(vectors, "space", [(i, i ^ 1) for i in range(count)])
    across = lax.ppermute(vectors, "space", outer)
    first = lax.axis_index("space") % 2 == 0
    return jnp.where(first, across, inside), jnp.where(first, inside, across)


def shifted(planes, by):
    length = planes.shape[-1]
    pad = [(0, 0)] * (planes.ndim - 1)
    if by > 0:
        return jnp.pad(planes[..., by:], pad + [(0, by)])
    return jnp.pad(planes[..., :length + by], pad + [(-by, 0)])


def coupling(vectors, low, high):
    z = jnp.arange(vectors.shape[-1]) % NZ
    nearest = shifted(vectors, NZ) + shifted(vectors, -NZ)
    second = shifted(vectors, 2 * NZ) + shifted(vectors, -2 * NZ)
    nearest = nearest + jnp.where(z >= 1, shifted(vectors, -1), 0.0)
    nearest = nearest + jnp.where(z <= NZ - 2, shifted(vectors, 1), 0.0)
    second = second + jnp.where(z >= 2, shifted(vectors, -2), 0.0)
    second = second + jnp.where(z <= NZ - 3, shifted(vectors, 2), 0.0)
    x = jnp.concatenate([low, vectors, high], axis=1)
    nearest = nearest + x[:, 1:3] + x[:, 3:5]
    second = second + x[:, 0:2] + x[:, 4:6]
    return second / 24.0 - 2.0 / 3.0 * nearest


def swapped(x, bits):
    return lax.ppermute(x, "band", [(i, i ^ bits) for i in range(lax.axis_size("band"))])


def pair_margins(product, lower, weight, beside=None):
    total = lax.psum(product, "space", axis_index_groups=SPACE_Z)
    total, beside = lax.optimization_barrier((total, beside))
    every = weight * copies(total, ("band", "space"), PAIR_PLANE)
    ahead, behind = jnp.sum(every[:8], axis=0), jnp.sum(every[8:], axis=0)
    return (jnp.where(lower, ahead, behind), jnp.where(lower, behind, ahead)), beside


def project_whole(parts, vectors, weight):
    product = jnp.concatenate([products(vectors, part) for part in parts], axis=1)
    margin = space_sum(product) * weight
    at = 0
    for part in parts:
        vectors = vectors - combination(margin[:, at : at + part.shape[0]], part)
        at += part.shape[0]
    return vectors


def on_device(occupied, initial, right_side, potential, energies):
    count, planes, line = initial.shape
    cells = planes * line
    weight = 1.0 / (lax.axis_size("space") * cells)
    tie = lax.optimization_barrier
    own = [states.reshape(-1, cells) for states in occupied]
    diagonal = 3.75 + potential[None, :, :] - energies[:, None, None]
    vectors = initial.reshape(count, cells)
    lower = lax.axis_index("band") % 4 < 2
    partner = swapped(vectors, 3)
    pair = jnp.concatenate(
        [jnp.where(lower, vectors, partner), jnp.where(lower, partner, vectors)], axis=0
    )
    run = copies(own[0], "band", BAND_Z).reshape(-1, cells)
    run, other, pair = tie((run, own[1], pair))
    across = swapped(run, 1)
    second = copies(other, "band", BAND_Z).reshape(-1, cells)
    near = jnp.concatenate([run, across], axis=0)
    margins, across = pair_margins(products(pair, near), lower, weight, swapped(second, 1))
    margins, far = tie((margins, swapped(near, 3)))
    first = (near, far)
    for margin, part in zip(margins, first):
        pair = pair - combination(margin, part)
    near = jnp.concatenate([second, across], axis=0)
    margins, _ = pair_margins(products(pair, near), lower, weight)
    margins, far = tie((margins, swapped(near, 3)))
    blocks = [first, (near, far)]
    vectors = jnp.where(lower, pair[:count], pair[count:])
    for margin, part in zip(margins, blocks[1]):
        vectors = vectors - combination(jnp.where(lower, margin[:count], margin[count:]), part)
    for iteration in range(ITERS):
        if iteration > 0:
            for block in blocks:
                vectors = project_whole(block, vectors, weight)
        low, high = neighbours(vectors)
        shape = (count, planes, line)
        vectors = vectors.reshape(shape)
        rest = right_side - coupling(vectors, low.reshape(shape), high.reshape(shape))
        residual = rest - diagonal * vectors
        vectors = (vectors + residual / diagonal).reshape(count, cells)
    return (vectors.reshape(shape), residual)


def solution(mesh):
    return jax.shard_map(
        on_device,
        mesh=mesh,
        in_specs=(
            P(None, "band", "space", None),
            P("band", "space", None),
            P("band", "space", None),
            P("space", None),
            P("band"),
        ),
        out_specs=(P("band", "space", None), P("band", "space", None)),
        check_vma=False,
    )
```

```python
import jax
import jax.numpy as jnp
from jax import lax
from jax.sharding import PartitionSpec as P

NZ = 32
ITERS = 2
BAND_Z = [[z * 4 + y for z in range(4)] for y in range(4)]
PAIR_PLANE = [
    [(z * 4 + y) * 32 + far * 8 + r for y in pair for r in range(8)]
    for z in range(4)
    for pair in ((0, 3), (1, 2))
    for far in range(4)
]
SPACE_PLANE = [[z * 8 + r for r in range(8)] for z in range(4)]
SPACE_Z = [[z * 8 + r for z in range(4)] for r in range(8)]


def copies(x, axis, groups):
    count = len(groups[0])
    sent = jnp.broadcast_to(x[None], (count,) + x.shape)
    return lax.all_to_all(sent, axis, 0, 0, axis_index_groups=groups)


def space_sum(x):
    near = jnp.sum(copies(x, "space", SPACE_PLANE), axis=0)
    return lax.psum(near, "space", axis_index_groups=SPACE_Z)


def products(vectors, states):
    return jnp.einsum(
        "vc,jc->vj",
        vectors,
        states,
        precision=lax.Precision.HIGH,
        preferred_element_type=jnp.float32,
    )


def combination(margin, states):
    return jnp.einsum(
        "vj,jc->vc",
        margin,
        states,
        precision=lax.Precision.HIGH,
        preferred_element_type=jnp.float32,
    )


def neighbours(vectors):
    count = lax.axis_size("space")
    outer = [(i, i + 1) for i in range(1, count - 1, 2)]
    outer = outer + [(j, i) for i, j in outer]
    across = lax.ppermute(vectors, "space", outer)
    both = lax.psum(vectors, "space", axis_index_groups=[[i, i + 1] for i in range(0, count, 2)])
    inside = both - vectors
    first = lax.axis_index("space") % 2 == 0
    return jnp.where(first, across, inside), jnp.where(first, inside, across)


def shifted(planes, by):
    length = planes.shape[-1]
    pad = [(0, 0)] * (planes.ndim - 1)
    if by > 0:
        return jnp.pad(planes[..., by:], pad + [(0, by)])
    return jnp.pad(planes[..., :length + by], pad + [(-by, 0)])


def coupling(vectors, low, high):
    z = jnp.arange(vectors.shape[-1]) % NZ
    nearest = shifted(vectors, NZ) + shifted(vectors, -NZ)
    second = shifted(vectors, 2 * NZ) + shifted(vectors, -2 * NZ)
    nearest = nearest + jnp.where(z >= 1, shifted(vectors, -1), 0.0)
    nearest = nearest + jnp.where(z <= NZ - 2, shifted(vectors, 1), 0.0)
    second = second + jnp.where(z >= 2, shifted(vectors, -2), 0.0)
    second = second + jnp.where(z <= NZ - 3, shifted(vectors, 2), 0.0)
    x = jnp.concatenate([low, vectors, high], axis=1)
    nearest = nearest + x[:, 1:3] + x[:, 3:5]
    second = second + x[:, 0:2] + x[:, 4:6]
    return second / 24.0 - 2.0 / 3.0 * nearest


def swapped(x, bits):
    return lax.ppermute(x, "band", [(i, i ^ bits) for i in range(lax.axis_size("band"))])


def pair_margins(product, lower, weight, beside=None, own_only=False):
    total = lax.psum(product, "space", axis_index_groups=SPACE_Z)
    total, beside = lax.optimization_barrier((total, beside))
    if own_only:
        count = product.shape[0] // 2
        rows = jnp.broadcast_to(total.reshape(2, 1, count, -1), (2, 8, count, total.shape[1]))
        every = weight * lax.all_to_all(
            rows.reshape(16, count, -1), ("band", "space"), 0, 0, axis_index_groups=PAIR_PLANE
        )
    else:
        every = weight * copies(total, ("band", "space"), PAIR_PLANE)
    ahead, behind = jnp.sum(every[:8], axis=0), jnp.sum(every[8:], axis=0)
    return (jnp.where(lower, ahead, behind), jnp.where(lower, behind, ahead)), beside


def project_whole(parts, vectors, weight):
    product = jnp.concatenate([products(vectors, part) for part in parts], axis=1)
    margin = space_sum(product) * weight
    at = 0
    for part in parts:
        vectors = vectors - combination(margin[:, at : at + part.shape[0]], part)
        at += part.shape[0]
    return vectors


def on_device(occupied, initial, right_side, potential, energies):
    count, planes, line = initial.shape
    cells = planes * line
    weight = 1.0 / (lax.axis_size("space") * cells)
    tie = lax.optimization_barrier
    own = [states.reshape(-1, cells) for states in occupied]
    diagonal = 3.75 + potential[None, :, :] - energies[:, None, None]
    vectors = initial.reshape(count, cells)
    lower = lax.axis_index("band") % 4 < 2
    partner = swapped(vectors, 3)
    pair = jnp.concatenate(
        [jnp.where(lower, vectors, partner), jnp.where(lower, partner, vectors)], axis=0
    )
    run = copies(own[0], "band", BAND_Z).reshape(-1, cells)
    run, other, pair = tie((run, own[1], pair))
    across = swapped(run, 1)
    second = copies(other, "band", BAND_Z).reshape(-1, cells)
    near = jnp.concatenate([run, across], axis=0)
    margins, across = pair_margins(products(pair, near), lower, weight, swapped(second, 1))
    margins, far = tie((margins, swapped(near, 3)))
    first = (near, far)
    for margin, part in zip(margins, first):
        pair = pair - combination(margin, part)
    near = jnp.concatenate([second, across], axis=0)
    margins, _ = pair_margins(products(pair, near), lower, weight, own_only=True)
    margins, far = tie((margins, swapped(near, 3)))
    blocks = [first, (near, far)]
    vectors = jnp.where(lower, pair[:count], pair[count:])
    for margin, part in zip(margins, blocks[1]):
        vectors = vectors - combination(margin, part)
    for iteration in range(ITERS):
        if iteration > 0:
            for block in blocks:
                vectors = project_whole(block, vectors, weight)
        low, high = neighbours(vectors)
        shape = (count, planes, line)
        vectors = vectors.reshape(shape)
        rest = right_side - coupling(vectors, low.reshape(shape), high.reshape(shape))
        residual = rest - diagonal * vectors
        vectors = (vectors + residual / diagonal).reshape(count, cells)
    return (vectors.reshape(shape), residual)


def solution(mesh):
    return jax.shard_map(
        on_device,
        mesh=mesh,
        in_specs=(
            P(None, "band", "space", None),
            P("band", "space", None),
            P("band", "space", None),
            P("space", None),
            P("band"),
        ),
        out_specs=(P("band", "space", None), P("band", "space", None)),
        check_vma=False,
    )
```

```python
import jax
import jax.numpy as jnp
from jax import lax
from jax.sharding import PartitionSpec as P

NZ = 32
ITERS = 2
BAND_Z = [[z * 4 + y for z in range(4)] for y in range(4)]
PAIR_PLANE = [
    [(z * 4 + y) * 32 + far * 8 + r for y in pair for r in range(8)]
    for z in range(4)
    for pair in ((0, 3), (1, 2))
    for far in range(4)
]
SPACE_PLANE = [[z * 8 + r for r in range(8)] for z in range(4)]
SPACE_Z = [[z * 8 + r for z in range(4)] for r in range(8)]


def copies(x, axis, groups):
    count = len(groups[0])
    sent = jnp.broadcast_to(x[None], (count,) + x.shape)
    return lax.all_to_all(sent, axis, 0, 0, axis_index_groups=groups)


def space_sum(x):
    near = jnp.sum(copies(x, "space", SPACE_PLANE), axis=0)
    return lax.psum(near, "space", axis_index_groups=SPACE_Z)


def products(vectors, states):
    return jnp.einsum(
        "vc,jc->vj",
        vectors,
        states,
        precision=lax.Precision.HIGH,
        preferred_element_type=jnp.float32,
    )


def combination(margin, states):
    return jnp.einsum(
        "vj,jc->vc",
        margin,
        states,
        precision=lax.Precision.HIGH,
        preferred_element_type=jnp.float32,
    )


def neighbours(vectors):
    count = lax.axis_size("space")
    outer = [(i, i + 1) for i in range(1, count - 1, 2)]
    outer = outer + [(j, i) for i, j in outer]
    inside = lax.ppermute(vectors, "space", [(i, i ^ 1) for i in range(count)])
    across = lax.ppermute(vectors, "space", outer)
    first = lax.axis_index("space") % 2 == 0
    return jnp.where(first, across, inside), jnp.where(first, inside, across)


def shifted(planes, by):
    length = planes.shape[-1]
    pad = [(0, 0)] * (planes.ndim - 1)
    if by > 0:
        return jnp.pad(planes[..., by:], pad + [(0, by)])
    return jnp.pad(planes[..., :length + by], pad + [(-by, 0)])


def coupling(vectors, low, high):
    z = jnp.arange(vectors.shape[-1]) % NZ
    nearest = shifted(vectors, NZ) + shifted(vectors, -NZ)
    second = shifted(vectors, 2 * NZ) + shifted(vectors, -2 * NZ)
    nearest = nearest + jnp.where(z >= 1, shifted(vectors, -1), 0.0)
    nearest = nearest + jnp.where(z <= NZ - 2, shifted(vectors, 1), 0.0)
    second = second + jnp.where(z >= 2, shifted(vectors, -2), 0.0)
    second = second + jnp.where(z <= NZ - 3, shifted(vectors, 2), 0.0)
    x = jnp.concatenate([low, vectors, high], axis=1)
    nearest = nearest + x[:, 1:3] + x[:, 3:5]
    second = second + x[:, 0:2] + x[:, 4:6]
    return second / 24.0 - 2.0 / 3.0 * nearest


def swapped(x, bits):
    return lax.ppermute(x, "band", [(i, i ^ bits) for i in range(lax.axis_size("band"))])


def pair_margins(product, lower, weight, beside=None, own_only=False):
    total = lax.psum(product, "space", axis_index_groups=SPACE_Z)
    total, beside = lax.optimization_barrier((total, beside))
    if own_only:
        count = product.shape[0] // 2
        rows = jnp.broadcast_to(total.reshape(2, 1, count, -1), (2, 8, count, total.shape[1]))
        every = weight * lax.all_to_all(
            rows.reshape(16, count, -1), ("band", "space"), 0, 0, axis_index_groups=PAIR_PLANE
        )
    else:
        every = weight * copies(total, ("band", "space"), PAIR_PLANE)
    ahead, behind = jnp.sum(every[:8], axis=0), jnp.sum(every[8:], axis=0)
    return (jnp.where(lower, ahead, behind), jnp.where(lower, behind, ahead)), beside


def project_whole(parts, vectors, weight):
    product = jnp.concatenate([products(vectors, part) for part in parts], axis=1)
    margin = space_sum(product) * weight
    at = 0
    for part in parts:
        vectors = vectors - combination(margin[:, at : at + part.shape[0]], part)
        at += part.shape[0]
    return vectors


def on_device(occupied, initial, right_side, potential, energies):
    count, planes, line = initial.shape
    cells = planes * line
    weight = 1.0 / (lax.axis_size("space") * cells)
    tie = lax.optimization_barrier
    own = [states.reshape(-1, cells) for states in occupied]
    diagonal = 3.75 + potential[None, :, :] - energies[:, None, None]
    vectors = initial.reshape(count, cells)
    lower = lax.axis_index("band") % 4 < 2
    partner = swapped(vectors, 3)
    pair = jnp.concatenate(
        [jnp.where(lower, vectors, partner), jnp.where(lower, partner, vectors)], axis=0
    )
    run = copies(own[0], "band", BAND_Z).reshape(-1, cells)
    run, other, pair = tie((run, own[1], pair))
    across = swapped(run, 1)
    second = copies(other, "band", BAND_Z).reshape(-1, cells)
    near = jnp.concatenate([run, across], axis=0)
    margins, across = pair_margins(products(pair, near), lower, weight, swapped(second, 1))
    margins, far = tie((margins, (swapped(run, 3), swapped(run, 2))))
    first = (near,) + far
    width = run.shape[0]
    columns = (margins[0], margins[1][:, :width], margins[1][:, width:])
    for margin, part in zip(columns, first):
        pair = pair - combination(margin, part)
    near = jnp.concatenate([second, across], axis=0)
    margins, _ = pair_margins(products(pair, near), lower, weight, own_only=True)
    margins, far = tie((margins, swapped(near, 3)))
    blocks = [first, (near, far)]
    vectors = jnp.where(lower, pair[:count], pair[count:])
    for margin, part in zip(margins, blocks[1]):
        vectors = vectors - combination(margin, part)
    for iteration in range(ITERS):
        if iteration > 0:
            for block in blocks:
                vectors = project_whole(block, vectors, weight)
        low, high = neighbours(vectors)
        shape = (count, planes, line)
        vectors = vectors.reshape(shape)
        rest = right_side - coupling(vectors, low.reshape(shape), high.reshape(shape))
        residual = rest - diagonal * vectors
        vectors = (vectors + residual / diagonal).reshape(count, cells)
    return (vectors.reshape(shape), residual)


def solution(mesh):
    return jax.shard_map(
        on_device,
        mesh=mesh,
        in_specs=(
            P(None, "band", "space", None),
            P("band", "space", None),
            P("band", "space", None),
            P("space", None),
            P("band"),
        ),
        out_specs=(P("band", "space", None), P("band", "space", None)),
        check_vma=False,
    )
```

```python
import jax
import jax.numpy as jnp
from jax import lax
from jax.sharding import PartitionSpec as P

NZ = 32
ITERS = 2
BAND_Z = [[z * 4 + y for z in range(4)] for y in range(4)]
PAIR_PLANE = [
    [(z * 4 + y) * 32 + far * 8 + r for y in pair for r in range(8)]
    for z in range(4)
    for pair in ((0, 3), (1, 2))
    for far in range(4)
]
SPACE_PLANE = [[z * 8 + r for r in range(8)] for z in range(4)]
SPACE_Z = [[z * 8 + r for z in range(4)] for r in range(8)]


def copies(x, axis, groups):
    count = len(groups[0])
    sent = jnp.broadcast_to(x[None], (count,) + x.shape)
    return lax.all_to_all(sent, axis, 0, 0, axis_index_groups=groups)


def space_sum(x):
    near = jnp.sum(copies(x, "space", SPACE_PLANE), axis=0)
    return lax.psum(near, "space", axis_index_groups=SPACE_Z)


def products(vectors, states):
    return jnp.einsum(
        "vc,jc->vj",
        vectors,
        states,
        precision=lax.Precision.HIGH,
        preferred_element_type=jnp.float32,
    )


def combination(margin, states):
    return jnp.einsum(
        "vj,jc->vc",
        margin,
        states,
        precision=lax.Precision.HIGH,
        preferred_element_type=jnp.float32,
    )


def neighbours(vectors):
    count = lax.axis_size("space")
    outer = [(i, i + 1) for i in range(1, count - 1, 2)]
    outer = outer + [(j, i) for i, j in outer]
    across = lax.ppermute(vectors, "space", outer)
    across, vectors = lax.optimization_barrier((across, vectors))
    inside = lax.ppermute(vectors, "space", [(i, i ^ 1) for i in range(count)])
    first = lax.axis_index("space") % 2 == 0
    return jnp.where(first, across, inside), jnp.where(first, inside, across)


def shifted(planes, by):
    length = planes.shape[-1]
    pad = [(0, 0)] * (planes.ndim - 1)
    if by > 0:
        return jnp.pad(planes[..., by:], pad + [(0, by)])
    return jnp.pad(planes[..., :length + by], pad + [(-by, 0)])


def coupling(vectors, low, high):
    z = jnp.arange(vectors.shape[-1]) % NZ
    nearest = shifted(vectors, NZ) + shifted(vectors, -NZ)
    second = shifted(vectors, 2 * NZ) + shifted(vectors, -2 * NZ)
    nearest = nearest + jnp.where(z >= 1, shifted(vectors, -1), 0.0)
    nearest = nearest + jnp.where(z <= NZ - 2, shifted(vectors, 1), 0.0)
    second = second + jnp.where(z >= 2, shifted(vectors, -2), 0.0)
    second = second + jnp.where(z <= NZ - 3, shifted(vectors, 2), 0.0)
    x = jnp.concatenate([low, vectors, high], axis=1)
    nearest = nearest + x[:, 1:3] + x[:, 3:5]
    second = second + x[:, 0:2] + x[:, 4:6]
    return second / 24.0 - 2.0 / 3.0 * nearest


def swapped(x, bits):
    return lax.ppermute(x, "band", [(i, i ^ bits) for i in range(lax.axis_size("band"))])


def pair_margins(product, lower, weight, beside=None, own_only=False):
    total = lax.psum(product, "space", axis_index_groups=SPACE_Z)
    total, beside = lax.optimization_barrier((total, beside))
    if own_only:
        count = product.shape[0] // 2
        rows = jnp.broadcast_to(total.reshape(2, 1, count, -1), (2, 8, count, total.shape[1]))
        every = weight * lax.all_to_all(
            rows.reshape(16, count, -1), ("band", "space"), 0, 0, axis_index_groups=PAIR_PLANE
        )
    else:
        every = weight * copies(total, ("band", "space"), PAIR_PLANE)
    ahead, behind = jnp.sum(every[:8], axis=0), jnp.sum(every[8:], axis=0)
    return (jnp.where(lower, ahead, behind), jnp.where(lower, behind, ahead)), beside


def project_whole(parts, vectors, weight):
    product = jnp.concatenate([products(vectors, part) for part in parts], axis=1)
    margin = space_sum(product) * weight
    at = 0
    for part in parts:
        vectors = vectors - combination(margin[:, at : at + part.shape[0]], part)
        at += part.shape[0]
    return vectors


def on_device(occupied, initial, right_side, potential, energies):
    count, planes, line = initial.shape
    cells = planes * line
    weight = 1.0 / (lax.axis_size("space") * cells)
    tie = lax.optimization_barrier
    own = [states.reshape(-1, cells) for states in occupied]
    diagonal = 3.75 + potential[None, :, :] - energies[:, None, None]
    vectors = initial.reshape(count, cells)
    lower = lax.axis_index("band") % 4 < 2
    partner = swapped(vectors, 3)
    pair = jnp.concatenate(
        [jnp.where(lower, vectors, partner), jnp.where(lower, partner, vectors)], axis=0
    )
    run = copies(own[0], "band", BAND_Z).reshape(-1, cells)
    run, other, pair = tie((run, own[1], pair))
    across = swapped(run, 1)
    second = copies(other, "band", BAND_Z).reshape(-1, cells)
    near = jnp.concatenate([run, across], axis=0)
    margins, across = pair_margins(products(pair, near), lower, weight, swapped(second, 1))
    margins, far = tie((margins, swapped(near, 3)))
    first = (near, far)
    for margin, part in zip(margins, first):
        pair = pair - combination(margin, part)
    near = jnp.concatenate([second, across], axis=0)
    margins, _ = pair_margins(products(pair, near), lower, weight, own_only=True)
    margins, far = tie((margins, swapped(near, 3)))
    blocks = [first, (near, far)]
    vectors = jnp.where(lower, pair[:count], pair[count:])
    for margin, part in zip(margins, blocks[1]):
        vectors = vectors - combination(margin, part)
    for iteration in range(ITERS):
        if iteration > 0:
            for block in blocks:
                vectors = project_whole(block, vectors, weight)
        low, high = neighbours(vectors)
        shape = (count, planes, line)
        vectors = vectors.reshape(shape)
        rest = right_side - coupling(vectors, low.reshape(shape), high.reshape(shape))
        residual = rest - diagonal * vectors
        vectors = (vectors + residual / diagonal).reshape(count, cells)
    return (vectors.reshape(shape), residual)


def solution(mesh):
    return jax.shard_map(
        on_device,
        mesh=mesh,
        in_specs=(
            P(None, "band", "space", None),
            P("band", "space", None),
            P("band", "space", None),
            P("space", None),
            P("band"),
        ),
        out_specs=(P("band", "space", None), P("band", "space", None)),
        check_vma=False,
    )
```

```python
import jax
import jax.numpy as jnp
from jax import lax
from jax.sharding import PartitionSpec as P

NZ = 32
ITERS = 2
BAND_Z = [[z * 4 + y for z in range(4)] for y in range(4)]
PAIR_PLANE = [
    [(z * 4 + y) * 32 + far * 8 + r for y in pair for r in range(8)]
    for z in range(4)
    for pair in ((0, 3), (1, 2))
    for far in range(4)
]
SPACE_PLANE = [[z * 8 + r for r in range(8)] for z in range(4)]
SPACE_Z = [[z * 8 + r for z in range(4)] for r in range(8)]


def copies(x, axis, groups):
    count = len(groups[0])
    sent = jnp.broadcast_to(x[None], (count,) + x.shape)
    return lax.all_to_all(sent, axis, 0, 0, axis_index_groups=groups)


def space_sum(x):
    near = jnp.sum(copies(x, "space", SPACE_PLANE), axis=0)
    return lax.psum(near, "space", axis_index_groups=SPACE_Z)


def products(vectors, states):
    return jnp.einsum(
        "vc,jc->vj",
        vectors,
        states,
        precision=lax.Precision.HIGH,
        preferred_element_type=jnp.float32,
    )


def combination(margin, states):
    return jnp.einsum(
        "vj,jc->vc",
        margin,
        states,
        precision=lax.Precision.HIGH,
        preferred_element_type=jnp.float32,
    )


def neighbours(vectors):
    count = lax.axis_size("space")
    outer = [(i, i + 1) for i in range(1, count - 1, 2)]
    outer = outer + [(j, i) for i, j in outer]
    across = lax.ppermute(vectors, "space", outer)
    across, vectors = lax.optimization_barrier((across, vectors))
    inside = lax.ppermute(vectors, "space", [(i, i ^ 1) for i in range(count)])
    first = lax.axis_index("space") % 2 == 0
    return jnp.where(first, across, inside), jnp.where(first, inside, across)


def shifted(planes, by):
    length = planes.shape[-1]
    pad = [(0, 0)] * (planes.ndim - 1)
    if by > 0:
        return jnp.pad(planes[..., by:], pad + [(0, by)])
    return jnp.pad(planes[..., :length + by], pad + [(-by, 0)])


def coupling(vectors, low, high):
    z = jnp.arange(vectors.shape[-1]) % NZ
    nearest = shifted(vectors, NZ) + shifted(vectors, -NZ)
    second = shifted(vectors, 2 * NZ) + shifted(vectors, -2 * NZ)
    nearest = nearest + jnp.where(z >= 1, shifted(vectors, -1), 0.0)
    nearest = nearest + jnp.where(z <= NZ - 2, shifted(vectors, 1), 0.0)
    second = second + jnp.where(z >= 2, shifted(vectors, -2), 0.0)
    second = second + jnp.where(z <= NZ - 3, shifted(vectors, 2), 0.0)
    x = jnp.concatenate([low, vectors, high], axis=1)
    nearest = nearest + x[:, 1:3] + x[:, 3:5]
    second = second + x[:, 0:2] + x[:, 4:6]
    return second / 24.0 - 2.0 / 3.0 * nearest


def swapped(x, bits):
    return lax.ppermute(x, "band", [(i, i ^ bits) for i in range(lax.axis_size("band"))])


def pair_margins(product, lower, weight, beside=None, own_only=False):
    total = lax.psum(product, "space", axis_index_groups=SPACE_Z)
    total, beside = lax.optimization_barrier((total, beside))
    if own_only:
        count = product.shape[0] // 2
        rows = jnp.broadcast_to(total.reshape(2, 1, count, -1), (2, 8, count, total.shape[1]))
        every = weight * lax.all_to_all(
            rows.reshape(16, count, -1), ("band", "space"), 0, 0, axis_index_groups=PAIR_PLANE
        )
    else:
        every = weight * copies(total, ("band", "space"), PAIR_PLANE)
    ahead, behind = jnp.sum(every[:8], axis=0), jnp.sum(every[8:], axis=0)
    return (jnp.where(lower, ahead, behind), jnp.where(lower, behind, ahead)), beside


def project_whole(parts, vectors, weight):
    product = jnp.concatenate([products(vectors, part) for part in parts], axis=1)
    margin = space_sum(product) * weight
    at = 0
    for part in parts:
        vectors = vectors - combination(margin[:, at : at + part.shape[0]], part)
        at += part.shape[0]
    return vectors


def on_device(occupied, initial, right_side, potential, energies):
    count, planes, line = initial.shape
    cells = planes * line
    weight = 1.0 / (lax.axis_size("space") * cells)
    tie = lax.optimization_barrier
    diagonal = 3.75 + potential[None, :, :] - energies[:, None, None]
    vectors = initial.reshape(count, cells)
    lower = lax.axis_index("band") % 4 < 2
    partner = swapped(vectors, 3)
    pair = jnp.concatenate(
        [jnp.where(lower, vectors, partner), jnp.where(lower, partner, vectors)], axis=0
    )
    run = copies(occupied[0].reshape(-1, cells), "band", BAND_Z).reshape(-1, cells)
    run, other, pair = tie((run, occupied[1], pair))
    across = swapped(run, 1)
    second = copies(other.reshape(-1, cells), "band", BAND_Z).reshape(-1, cells)
    near = jnp.concatenate([run, across], axis=0)
    margins, across = pair_margins(products(pair, near), lower, weight, swapped(second, 1))
    margins, far = tie((margins, swapped(near, 3)))
    first = (near, far)
    for margin, part in zip(margins, first):
        pair = pair - combination(margin, part)
    near = jnp.concatenate([second, across], axis=0)
    margins, _ = pair_margins(products(pair, near), lower, weight, own_only=True)
    margins, far = tie((margins, swapped(near, 3)))
    blocks = [first, (near, far)]
    vectors = jnp.where(lower, pair[:count], pair[count:])
    for margin, part in zip(margins, blocks[1]):
        vectors = vectors - combination(margin, part)
    for iteration in range(ITERS):
        if iteration > 0:
            for block in blocks:
                vectors = project_whole(block, vectors, weight)
        low, high = neighbours(vectors)
        shape = (count, planes, line)
        vectors = vectors.reshape(shape)
        rest = right_side - coupling(vectors, low.reshape(shape), high.reshape(shape))
        residual = rest - diagonal * vectors
        vectors = (vectors + residual / diagonal).reshape(count, cells)
    return (vectors.reshape(shape), residual)


def solution(mesh):
    return jax.shard_map(
        on_device,
        mesh=mesh,
        in_specs=(
            P(None, "band", "space", None),
            P("band", "space", None),
            P("band", "space", None),
            P("space", None),
            P("band"),
        ),
        out_specs=(P("band", "space", None), P("band", "space", None)),
        check_vma=False,
    )
```
